256 devices in a mesh: view: 8 (over x, core), samp: 32 (over z, y).
Axes of the slice: x: 4, y: 4, z: 8, core: 2. Of those that a mesh axis runs over, the one named last changes fastest.
Arguments:
- view_data: bfloat16 [16, 16384, 2048], P('view', 'samp'), may hold values from -10 to 10
- init_coeffs: float32 [16, 2048, 128], P('view'), may hold values from -0.125 to 0.125
Outputs:
- shared_scores: float32 [16384, 128], P('samp')
- final_coeffs: float32 [16, 2048, 128], P('view', 'samp')
The draws below stay inside these ranges and needn't reach their ends.
All inputs are finite; a program needn't handle non-finite values.
Results may differ from the reference program's by a relative error of at most 0.005.
Values may be sent and summed in bfloat16 or wider, within the bound.
A program may use at most 128 MiB of HBM per device.

```python
import jax
import jax.numpy as jnp
from jax import lax

F = 2048
K = 128
OUTER = 2
INNER = 2
NS_ITERS = 12
VIEWS = 16
NSAMP = 16384


def draw_view_data(key, part):
    key_feat = jax.random.fold_in(key, 11)
    key_noise = jax.random.fold_in(key, 23)
    top = 10.0
    feat = jax.random.uniform(key_feat, (VIEWS, 1, F), jnp.float32)
    where = (jnp.arange(NSAMP, dtype=jnp.float32) + 0.5) / NSAMP
    rate = 2.0 * jnp.log(top) * feat
    safe_rate = jnp.maximum(rate, 0.0001)
    mean_square = jnp.where(rate > 0.0001, jnp.expm1(safe_rate) / safe_rate, 1.0 + 0.5 * rate)
    growth = jnp.exp(0.5 * rate * where[None, :, None]) / jnp.sqrt(mean_square)
    noise = jnp.clip(jax.random.normal(key_noise, (VIEWS, NSAMP, F), jnp.float32), -4.0, 4.0)
    return (noise * growth).astype(jnp.bfloat16)


def shard_levels(rng, dims, split, low, top_value):
    factor_of, own = 1.0, jax.random.fold_in(rng, 6)
    for dim, blocks in split:
        draws = jnp.exp(jax.random.uniform(jax.random.fold_in(own, dim), (blocks,), jnp.float32, low / len(split), top_value / len(split)))
        factor_of = factor_of * jnp.repeat(draws, dims[dim] // blocks).reshape([-1 if axis == dim else 1 for axis in range(len(dims))])
    return factor_of


def gaussian(stream_key, shape, spread, most, cuts=(), held_as=jnp.bfloat16):
    result = jax.random.normal(stream_key, shape, jnp.float32) * spread
    if len(cuts) > 0:
        result = shard_levels(stream_key, shape, cuts, -0.22, 0.18) * result
    return jnp.clip(result, min=-most, max=most).astype(held_as)


def setup_inputs(seed: int = 0) -> dict:
    splits = jax.random.split(jax.random.key(seed), 3)
    return {
        "view_data": draw_view_data(jax.random.fold_in(splits[2], 71), 0),
        "init_coeffs": gaussian(splits[1], (VIEWS, F, K), F ** -0.5, 0.125, ((0, 8),), jnp.float32),
    }


HIGH = lax.Precision.HIGHEST
ridge_weight = 0.1
step_size = 0.5

def newton_inverse(gram):
    size_k = gram.shape[0]
    eye_mat = jnp.eye(size_k, dtype=jnp.float32)
    shrunk = gram + jnp.trace(gram) / size_k * eye_mat
    scale = jnp.sqrt(jnp.sum(shrunk * shrunk))
    approx = shrunk / scale
    inverse = eye_mat
    for turn in range(NS_ITERS):
        factor = 0.5 * (3.0 * eye_mat - jnp.dot(inverse, approx, precision=HIGH))
        approx = jnp.dot(approx, factor, precision=HIGH)
        inverse = jnp.dot(factor, inverse, precision=HIGH)
    return (inverse, scale)

def make_scores(view_data, coeffs):
    summed = jnp.zeros((view_data.shape[1], coeffs.shape[2]), jnp.float32)
    for member in range(view_data.shape[0]):
        summed = summed + jnp.dot(view_data[member], coeffs[member].astype(jnp.bfloat16), preferred_element_type=jnp.float32)
    gram = jnp.dot(summed.T, summed, precision=HIGH)
    inverse, scale = newton_inverse(gram)
    return jnp.dot(summed, inverse, precision=HIGH) * jnp.sqrt(view_data.shape[1] / scale)

def reference(view_data, init_coeffs):
    total = view_data.shape[1]
    coeffs = init_coeffs
    scores = make_scores(view_data, coeffs)
    for outer_step in range(OUTER):
        for inner_step in range(INNER):
            updated = []
            for member in range(view_data.shape[0]):
                weights = coeffs[member]
                resid = (jnp.dot(view_data[member], weights.astype(jnp.bfloat16), preferred_element_type=jnp.float32) - scores).astype(jnp.bfloat16)
                term = lax.dot_general(view_data[member], resid, (((0,), (0,)), ((), ())), preferred_element_type=jnp.float32)
                grad = term / total + ridge_weight * weights
                updated.append(weights - step_size * grad)
            coeffs = jnp.stack(updated)
        scores = make_scores(view_data, coeffs)
    return (scores, coeffs)
```

```python
import functools

import jax
import jax.numpy as jnp
from jax import lax
from jax.experimental import pallas as pl
from jax.experimental.pallas import tpu as pltpu
from jax.sharding import PartitionSpec as P

OUTER = 2
NS_ITERS = 12
RIDGE = 0.1
STEP = 0.5

HIGH = lax.Precision.HIGHEST
MESH = pl.DeviceIdType.MESH
F32 = jnp.float32
BF16 = jnp.bfloat16

NX, NC, NY, NZ = 4, 2, 4, 8
VIEWS, ROWS, FEATS, K = 2, 512, 2048, 128
BLOCK = FEATS // NZ
OWN = BLOCK // NY
MAIN, REST = 48, 16
SAMPLES = ROWS * NY * NZ
GROWS = K // (NX * NC)
SROWS = ROWS // (NX * NC)


def dot32(a, b):
    return jnp.dot(a, b, precision=HIGH, preferred_element_type=F32)


def dot16(a, b):
    return jnp.dot(a, b, preferred_element_type=F32)


def far_first(i):
    odd = lax.rem(i, 2)
    return lax.rem(4 + odd * ((i + 1) // 2) - (1 - odd) * (i // 2), NZ)


def kernel(
    x_ref, w_ref, scores_ref, coeffs_ref,
    xt, wb, gb, p, pb, sb, wrow, bm, ga,
    vloc, vin, summed, gram, gpart, gyin, gzout, gzin,
    ryin, szout, rz2in, rz1in, syout, ry2in,
    vrs_s, vrs_r, vag_s, vag_r, gy_s, gy_r, gz_s, gz_r, gv_s, gv_r,
    ry_s, ry_r, rz2_s, rz2_r, rz1_s, rz1_r, ry2_s, ry2_r,
    az_s, az_r, ayf_s, ayf_r, ay_s, ay_r, az2_s, az2_r,
):
    v = lax.axis_index("view")
    s = lax.axis_index("samp")
    y, z = lax.rem(s, NY), s // NY

    def y_peer(m):
        return {"view": v, "samp": z * NY + lax.rem(y + m, NY)}

    def z_peer(j):
        return {"view": v, "samp": lax.rem(z + j, NZ) * NY + y}

    def v_peer(j):
        return {"view": lax.rem(v + j, NX * NC), "samp": s}

    def copy(src, dst, send, recv, device):
        return pltpu.make_async_remote_copy(
            src_ref=src, dst_ref=dst, send_sem=send, recv_sem=recv, device_id=device, device_id_type=MESH
        )

    barrier = pltpu.get_barrier_semaphore()
    for m in range(1, NY):
        pl.semaphore_signal(barrier, inc=1, device_id=y_peer(m), device_id_type=MESH)
    for j in range(1, NZ):
        pl.semaphore_signal(barrier, inc=1, device_id=z_peer(j), device_id_type=MESH)
    for j in range(1, NX * NC):
        pl.semaphore_signal(barrier, inc=1, device_id=v_peer(j), device_id_type=MESH)

    def vrs_copy(t, j):
        to = lax.rem(v + j, NX * NC)
        return copy(vloc.at[t, to], vin.at[t, j], vrs_s.at[t, j], vrs_r.at[t, j], v_peer(j))

    def vag_copy(t, j):
        block = summed.at[t, pl.ds(v * SROWS, SROWS)]
        return copy(block, block, vag_s.at[t, j], vag_r.at[t, j], v_peer(j))

    def vrs_start(t):
        vloc[t] = (p[0] + p[1]).reshape(NX * NC, SROWS, K).astype(vloc.dtype)
        for j in range(1, NX * NC):
            vrs_copy(t, j).start()

    def vrs_end(t):
        total = vloc[t, v].astype(F32)
        for j in range(1, NX * NC):
            vrs_copy(t, j).wait()
            total = total + vin[t, j].astype(F32)
        summed[t, pl.ds(v * SROWS, SROWS)] = total
        for j in range(1, NX * NC):
            vag_copy(t, j).start()

    def vag_end(t):
        for j in range(1, NX * NC):
            vag_copy(t, j).wait()

    def gy_copy(t, m):
        return copy(gpart.at[t, v], gyin.at[t, m], gy_s.at[t, m], gy_r.at[t, m], y_peer(m))

    def gz_copy(t, j):
        return copy(gzout.at[t], gzin.at[t, j], gz_s.at[t, j], gz_r.at[t, j], z_peer(j))

    def gv_copy(t, j):
        block = gram.at[t, pl.ds(v * GROWS, GROWS)]
        return copy(block, block, gv_s.at[t, j], gv_r.at[t, j], v_peer(j))

    def gram_start(t):
        everyone = summed[t]
        gpart[t] = dot32(everyone.T, everyone).reshape(NX * NC, GROWS, K)
        for m in range(1, NY):
            gy_copy(t, m).start()

    def gram_y_end(t):
        total = gpart[t, v]
        for m in range(1, NY):
            gy_copy(t, m).wait()
            total = total + gyin[t, m]
        gzout[t] = total
        for j in range(1, NZ):
            gz_copy(t, j).start()

    def gram_z_end(t):
        total = gzout[t]
        for j in range(1, NZ):
            gz_copy(t, j).wait()
            total = total + gzin[t, j]
        gram[t, pl.ds(v * GROWS, GROWS)] = total
        for j in range(1, NX * NC):
            gv_copy(t, j).start()

    def gram_end(t):
        for j in range(1, NX * NC):
            gv_copy(t, j).wait()

    def eye_mat():
        row = lax.broadcasted_iota(jnp.int32, (K, K), 0)
        col = lax.broadcasted_iota(jnp.int32, (K, K), 1)
        return jnp.where(row == col, 1.0, 0.0).astype(F32)

    def newton_init(t):
        eye = eye_mat()
        full = gram[t]
        trace = jnp.sum(full * eye, keepdims=True)
        shrunk = full + trace / K * eye
        scale = jnp.sqrt(jnp.sum(shrunk * shrunk, keepdims=True))
        return shrunk / scale, eye, scale

    def newton_turns(approx, inverse, turns):
        eye = eye_mat()

        def turn(_, both):
            approx, inverse = both[:, :K], both[:, K:]
            factor = 0.5 * (3.0 * eye - dot32(inverse, approx))
            return dot32(factor, both)

        both = lax.fori_loop(0, turns, turn, jnp.concatenate([approx, inverse], axis=1))
        return both[:, :K], both[:, K:]

    def ry_copy(r, j, m):
        to_z, to_y = lax.rem(z + j, NZ), lax.rem(y + m, NY)
        return copy(
            gb.at[r, :, to_z, to_y, pl.ds(0, MAIN)], ryin.at[r, j, m], ry_s.at[r, j, m], ry_r.at[r, j, m], y_peer(m)
        )

    def rz1_copy(r, j):
        to_z = lax.rem(z + j, NZ)
        return copy(
            gb.at[r, :, to_z, :, pl.ds(MAIN, REST)], rz1in.at[r, j], rz1_s.at[r, j], rz1_r.at[r, j], z_peer(j)
        )

    def rz2_copy(r, j):
        return copy(szout.at[r, j], rz2in.at[r, j], rz2_s.at[r, j], rz2_r.at[r, j], z_peer(j))

    def ry2_copy(r, m):
        to_y = lax.rem(y + m, NY)
        return copy(syout.at[r, to_y], ry2in.at[r, m], ry2_s.at[r, m], ry2_r.at[r, m], y_peer(m))

    def rs_start(r, right):
        def step(i, _):
            j = far_first(i)
            to_z = lax.rem(z + j, NZ)
            rows = pl.ds(pl.multiple_of(to_z * BLOCK, BLOCK), BLOCK)
            for member in range(VIEWS):
                block = dot16(xt[member, rows, :], right(member))
                gb[r, member, to_z] = block.astype(BF16).reshape(NY, OWN, K)
            for m in range(1, NY):
                ry_copy(r, j, m).start()

            @pl.when(i < NZ - 1)
            def _():
                rz1_copy(r, j).start()

            return 0

        lax.fori_loop(0, NZ, step, 0)

    def rs_mid(r):
        def step(i, _):
            j = far_first(i)
            to_z = lax.rem(z + j, NZ)
            total = gb[r, :, to_z, y, 0:MAIN].astype(F32)
            for m in range(1, NY):
                ry_copy(r, j, m).wait()
                total = total + ryin[r, j, m].astype(F32)
            szout[r, j] = total.astype(BF16)

            @pl.when(i < NZ - 1)
            def _():
                rz2_copy(r, j).start()

            return 0

        lax.fori_loop(0, NZ, step, 0)
        total = gb[r, :, z, :, MAIN:OWN].astype(F32)
        for j in range(1, NZ):
            rz1_copy(r, j).wait()
            total = total + rz1in[r, j].astype(F32)
        for to in range(NY):
            syout[r, to] = total[:, to].astype(BF16)
        for m in range(1, NY):
            ry2_copy(r, m).start()

    def rs_end(r):
        total = syout[r, y].astype(F32)
        for m in range(1, NY):
            ry2_copy(r, m).wait()
            total = total + ry2in[r, m].astype(F32)
        ga[:, MAIN:OWN] = total
        total = szout[r, 0].astype(F32)
        for j in range(1, NZ):
            rz2_copy(r, j).wait()
            total = total + rz2in[r, j].astype(F32)
        ga[:, 0:MAIN] = total

    def az_copy(a, j):
        block = wb.at[a, :, z, y, pl.ds(0, MAIN)]
        return copy(block, block, az_s.at[a, j], az_r.at[a, j], z_peer(j))

    def ayf_copy(a, j, m):
        from_z = lax.rem(z - j + NZ, NZ)
        block = wb.at[a, :, from_z, y, pl.ds(0, MAIN)]
        return copy(block, block, ayf_s.at[a, j, m], ayf_r.at[a, j, m], y_peer(m))

    def ay_copy(a, m):
        block = wb.at[a, :, z, y, pl.ds(MAIN, REST)]
        return copy(block, block, ay_s.at[a, m], ay_r.at[a, m], y_peer(m))

    def az2_copy(a, j):
        block = wb.at[a, :, z, :, pl.ds(MAIN, REST)]
        return copy(block, block, az2_s.at[a, j], az2_r.at[a, j], z_peer(j))

    def gather_start(a):
        wb[a, :, z, y] = wrow[...].astype(BF16)
        for m in range(1, NY):
            ay_copy(a, m).start()
        for j in (1, 7, 2, 6, 3, 5, 4):
            az_copy(a, j).start()
        for m in range(1, NY):
            ayf_copy(a, 0, m).start()

    def gather_products(a):
        for m in range(1, NY):
            ay_copy(a, m).wait()
        for j in (4, 5, 3, 6, 2, 7, 1):
            az2_copy(a, j).start()

        def forward(i, _):
            j = far_first(NZ - 1 - i)
            az_copy(a, j).wait()
            for m in range(1, NY):
                ayf_copy(a, j, m).start()
            return 0

        lax.fori_loop(1, NZ, forward, 0)

        p[...] = jnp.zeros_like(p)

        def product(i, _):
            j = far_first(NZ - 1 - i)
            from_z = lax.rem(z - j + NZ, NZ)
            for m in range(1, NY):
                ayf_copy(a, j, m).wait()

            @pl.when(i > 0)
            def _():
                az2_copy(a, j).wait()

            product_of(a, from_z)
            return 0

        lax.fori_loop(0, NZ, product, 0)

    def product_of(a, from_z):
        cols = pl.ds(pl.multiple_of(from_z * BLOCK, BLOCK), BLOCK)
        for member in range(VIEWS):
            p[member] += dot16(x_ref[member, :, cols], wb[a, member, from_z].reshape(BLOCK, K))

    def update():
        grad = (ga[...].reshape(VIEWS * OWN, K) - bm[...]) / SAMPLES
        old = wrow[...].reshape(VIEWS * OWN, K)
        wrow[...] = (old - STEP * (grad + RIDGE * old)).reshape(VIEWS, OWN, K)

    wb[0] = w_ref[...].reshape(VIEWS, NZ, NY, OWN, K).astype(BF16)
    wrow[...] = w_ref[:, pl.ds(pl.multiple_of(s * OWN, OWN), OWN), :]
    p[...] = jnp.zeros_like(p)

    def first(i, _):
        product_of(0, i)
        return 0

    lax.fori_loop(0, NZ, first, 0)
    pl.semaphore_wait(barrier, (NY - 1) + (NZ - 1) + (NX * NC - 1))

    def turn_over(i, _):
        cols = pl.ds(pl.multiple_of(i * BLOCK, BLOCK), BLOCK)
        for member in range(VIEWS):
            xt[member, cols, :] = x_ref[member, :, cols].T
        return 0

    lax.fori_loop(0, NZ, turn_over, 0)

    def outer(o, _):
        own_r, sum_r, next_r = 3 * o, 3 * o + 1, 3 * o + 2
        vrs_start(o)
        pb[...] = p[...].astype(BF16)
        rs_start(own_r, lambda member: pb[member])
        vrs_end(o)
        vag_end(o)
        gram_start(o)
        sb[...] = summed[o].astype(BF16)
        gram_y_end(o)
        rs_mid(own_r)
        rs_start(sum_r, lambda member: sb[...])
        gram_z_end(o)
        rs_end(own_r)
        gram_end(o)
        approx, inverse, scale = newton_init(o)
        approx, inverse = newton_turns(approx, inverse, NS_ITERS // 2)
        rs_mid(sum_r)
        approx, inverse = newton_turns(approx, inverse, NS_ITERS - NS_ITERS // 2)
        white = inverse * jnp.sqrt(SAMPLES / scale)
        grad_own = ga[...]
        rs_end(sum_r)
        bm[...] = dot32(ga[...].reshape(VIEWS * OWN, K), white)
        ga[...] = grad_own
        update()
        gather_start(2 * o + 1)
        gather_products(2 * o + 1)
        pb[...] = p[...].astype(BF16)
        rs_start(next_r, lambda member: pb[member])
        rs_mid(next_r)
        rs_end(next_r)
        update()
        gather_start(2 * o + 2)
        gather_products(2 * o + 2)
        return 0

    lax.fori_loop(0, OUTER, outer, 0)
    vrs_start(OUTER)
    coeffs_ref[...] = wrow[...]
    vrs_end(OUTER)
    vag_end(OUTER)
    gram_start(OUTER)
    gram_y_end(OUTER)
    gram_z_end(OUTER)
    gram_end(OUTER)
    approx, inverse, scale = newton_init(OUTER)
    approx, inverse = newton_turns(approx, inverse, NS_ITERS)
    scores_ref[...] = dot32(summed[OUTER], inverse * jnp.sqrt(SAMPLES / scale))


def body(view_data, init_coeffs):
    evals, reduces, gathers = OUTER + 1, 3 * OUTER, 2 * OUTER
    peers = NX * NC
    vmem, dma = pltpu.VMEM, pltpu.SemaphoreType.DMA
    scratch = [
        vmem((VIEWS, FEATS, ROWS), BF16),
        vmem((gathers + 1, VIEWS, NZ, NY, OWN, K), BF16),
        vmem((reduces, VIEWS, NZ, NY, OWN, K), BF16),
        vmem((VIEWS, ROWS, K), F32),
        vmem((VIEWS, ROWS, K), BF16),
        vmem((ROWS, K), BF16),
        vmem((VIEWS, OWN, K), F32),
        vmem((VIEWS * OWN, K), F32),
        vmem((VIEWS, OWN, K), F32),
        vmem((evals, peers, SROWS, K), BF16),
        vmem((evals, peers, SROWS, K), BF16),
        vmem((evals, ROWS, K), F32),
        vmem((evals, K, K), F32),
        vmem((evals, peers, GROWS, K), F32),
        vmem((evals, NY, GROWS, K), F32),
        vmem((evals, GROWS, K), F32),
        vmem((evals, NZ, GROWS, K), F32),
        vmem((reduces, NZ, NY, VIEWS, MAIN, K), BF16),
        vmem((reduces, NZ, VIEWS, MAIN, K), BF16),
        vmem((reduces, NZ, VIEWS, MAIN, K), BF16),
        vmem((reduces, NZ, VIEWS, NY, REST, K), BF16),
        vmem((reduces, NY, VIEWS, REST, K), BF16),
        vmem((reduces, NY, VIEWS, REST, K), BF16),
    ]
    for shape in (
        (evals, peers), (evals, peers), (evals, NY), (evals, NZ), (evals, peers),
        (reduces, NZ, NY), (reduces, NZ), (reduces, NZ), (reduces, NY),
        (gathers + 1, NZ), (gathers + 1, NZ, NY), (gathers + 1, NY), (gathers + 1, NZ),
    ):
        scratch += [dma(shape), dma(shape)]
    return pl.pallas_call(
        kernel,
        out_shape=(jax.ShapeDtypeStruct((ROWS, K), F32), jax.ShapeDtypeStruct((VIEWS, OWN, K), F32)),
        in_specs=[pl.BlockSpec(memory_space=pltpu.VMEM)] * 2,
        out_specs=(pl.BlockSpec(memory_space=pltpu.VMEM),) * 2,
        scratch_shapes=scratch,
        compiler_params=pltpu.CompilerParams(collective_id=0, has_side_effects=True, vmem_limit_bytes=56 << 20),
        name="gcca",
    )(view_data, init_coeffs)


def solution(mesh):
    in_specs = (P("view", "samp", None), P("view", None, None))
    out_specs = (P("samp", None), P("view", "samp", None))
    return jax.shard_map(body, mesh=mesh, in_specs=in_specs, out_specs=out_specs, check_vma=False)
```

```python
import functools

import jax
import jax.numpy as jnp
from jax import lax
from jax.experimental import pallas as pl
from jax.experimental.pallas import tpu as pltpu
from jax.sharding import PartitionSpec as P

OUTER = 2
NS_ITERS = 12
RIDGE = 0.1
STEP = 0.5

HIGH = lax.Precision.HIGHEST
MESH = pl.DeviceIdType.MESH
F32 = jnp.float32
BF16 = jnp.bfloat16

NX, NC, NY, NZ = 4, 2, 4, 8
VIEWS, ROWS, FEATS, K = 2, 512, 2048, 128
BLOCK = FEATS // NZ
OWN = BLOCK // NY
MAIN, REST = 48, 16
SAMPLES = ROWS * NY * NZ
PEERS = NX * NC
SENT = (NY * NZ - 1) * OWN * K // ROWS
GROWS = K // (NX * NC)
SROWS = ROWS // (NX * NC)


def dot32(a, b):
    return jnp.dot(a, b, precision=HIGH, preferred_element_type=F32)


def dot16(a, b):
    return jnp.dot(a, b, preferred_element_type=F32)


def far_first(i):
    odd = lax.rem(i, 2)
    return lax.rem(4 + odd * ((i + 1) // 2) - (1 - odd) * (i // 2), NZ)


def kernel(
    x_ref, w_ref, scores_ref, coeffs_ref,
    xt, wb, gb, p, pb, sb, wrow, bm, ga, gs,
    vloc, vin, summed, gram, gpart, gvin, gyout, gyin, gzout, gzin,
    ryin, szout, rz2in, rz1in, syout, ry2in,
    vrs_r, vag_r, gx_r, gy_r, gz_r, gv_r, vrs_s, vag_s, gram_s,
    ry_r, rz2_r, rz1_r, ry2_r, rs_s,
    az_r, ayf_r, ay_r, az2_r, ag_s,
):
    v = lax.axis_index("view")
    s = lax.axis_index("samp")
    y, z = lax.rem(s, NY), s // NY

    def y_peer(m):
        return {"view": v, "samp": z * NY + lax.rem(y + m, NY)}

    def z_peer(j):
        return {"view": v, "samp": lax.rem(z + j, NZ) * NY + y}

    def v_peer(j):
        return {"view": lax.rem(v + j, PEERS), "samp": s}

    def copy(src, dst, send, recv, device):
        return pltpu.make_async_remote_copy(
            src_ref=src, dst_ref=dst, send_sem=send, recv_sem=recv, device_id=device, device_id_type=MESH
        )

    def arrived(ref, recv):
        copy(ref, ref, ag_s.at[0], recv, y_peer(1)).wait_recv()

    def sent(ref, send):
        copy(ref, ref, send, ay_r.at[0], y_peer(1)).wait_send()

    barrier = pltpu.get_barrier_semaphore()
    for m in range(1, NY):
        pl.semaphore_signal(barrier, inc=1, device_id=y_peer(m), device_id_type=MESH)
    for j in range(1, NZ):
        pl.semaphore_signal(barrier, inc=1, device_id=z_peer(j), device_id_type=MESH)
    for j in range(1, PEERS):
        pl.semaphore_signal(barrier, inc=1, device_id=v_peer(j), device_id_type=MESH)

    def vrs_start(t):
        vloc[t] = (p[0] + p[1]).reshape(PEERS, SROWS, K).astype(vloc.dtype)
        for j in range(1, PEERS):
            to = lax.rem(v + j, PEERS)
            copy(vloc.at[t, to], vin.at[t, j], vrs_s.at[0], vrs_r.at[0], v_peer(j)).start()

    def vrs_end(t):
        total = vloc[t, v].astype(F32)
        arrived(vin.at[t, pl.ds(1, PEERS - 1)], vrs_r.at[0])
        for j in range(1, PEERS):
            total = total + vin[t, j].astype(F32)
        summed[t, pl.ds(v * SROWS, SROWS)] = total
        gpart[t] = dot32(total.T, total).reshape(PEERS, GROWS, K)
        for j in range(1, PEERS):
            to = lax.rem(v + j, PEERS)
            copy(gpart.at[t, to], gvin.at[t, j], gram_s.at[0], gx_r.at[0], v_peer(j)).start()
        block = summed.at[t, pl.ds(v * SROWS, SROWS)]
        for j in range(1, PEERS):
            copy(block, block, vag_s.at[0], vag_r.at[0], v_peer(j)).start()

    def vag_end(t):
        arrived(summed.at[t, pl.ds(0, ROWS - SROWS)], vag_r.at[0])

    def gram_v_end(t):
        total = gpart[t, v]
        arrived(gvin.at[t, pl.ds(1, PEERS - 1)], gx_r.at[0])
        for j in range(1, PEERS):
            total = total + gvin[t, j]
        gyout[t] = total
        for m in range(1, NY):
            copy(gyout.at[t], gyin.at[t, m], gram_s.at[0], gy_r.at[0], y_peer(m)).start()

    def gram_y_end(t):
        total = gyout[t]
        arrived(gyin.at[t, pl.ds(1, NY - 1)], gy_r.at[0])
        for m in range(1, NY):
            total = total + gyin[t, m]
        gzout[t] = total
        for j in (4, 5, 3, 6, 2, 7, 1):
            copy(gzout.at[t], gzin.at[t, j], gram_s.at[0], gz_r.at[0], z_peer(j)).start()

    def gram_z_end(t):
        total = gzout[t]
        arrived(gzin.at[t, pl.ds(1, NZ - 1)], gz_r.at[0])
        for j in range(1, NZ):
            total = total + gzin[t, j]
        gram[t, pl.ds(v * GROWS, GROWS)] = total
        block = gram.at[t, pl.ds(v * GROWS, GROWS)]
        for j in range(1, PEERS):
            copy(block, block, gram_s.at[0], gv_r.at[0], v_peer(j)).start()

    def gram_end(t):
        arrived(gram.at[t, pl.ds(0, K - GROWS)], gv_r.at[0])
        sent(vin.at[t, pl.ds(1, PEERS - 1)], vrs_s.at[0])
        sent(summed.at[t, pl.ds(0, ROWS - SROWS)], vag_s.at[0])
        sent(summed.at[t, pl.ds(0, (3 * 7 + 3) * GROWS)], gram_s.at[0])

    def eye_mat():
        row = lax.broadcasted_iota(jnp.int32, (K, K), 0)
        col = lax.broadcasted_iota(jnp.int32, (K, K), 1)
        return jnp.where(row == col, 1.0, 0.0).astype(F32)

    def newton_init(t):
        eye = eye_mat()
        full = gram[t]
        trace = jnp.sum(full * eye, keepdims=True)
        shrunk = full + trace / K * eye
        scale = jnp.sqrt(jnp.sum(shrunk * shrunk, keepdims=True))
        return jnp.concatenate([shrunk / scale, eye], axis=1), scale

    def newton_turns(first, last, both, beside=None):
        eye = eye_mat()

        def turn(i, both):
            approx, inverse = both[:, :K], both[:, K:]
            factor = 0.5 * (3.0 * eye - dot32(inverse, approx))
            both = dot32(factor, both)
            if beside is not None:
                beside(i)
            return both

        return lax.fori_loop(first, last, turn, both)

    def ry_start(r, q, member, j):
        to_z = lax.rem(z + j, NZ)
        for m in range(1, NY):
            to_y = lax.rem(y + m, NY)
            copy(
                gb.at[r, member, to_z, to_y, pl.ds(0, MAIN)], ryin.at[r, member, j, m],
                rs_s.at[q, member], ry_r.at[q, member, j], y_peer(m),
            ).start()

    def rz1_start(r, q, member, j):
        to_z = lax.rem(z + j, NZ)
        copy(
            gb.at[r, member, to_z, :, pl.ds(MAIN, REST)], rz1in.at[r, member, j],
            rs_s.at[q, member], rz1_r.at[q, member], z_peer(j),
        ).start()

    def rs_start(r, q, member, right, both_orders=True):
        def step(i, _):
            j = far_first(i)
            to_z = lax.rem(z + j, NZ)
            rows = pl.ds(pl.multiple_of(to_z * BLOCK, BLOCK), BLOCK)
            block = dot16(xt[member, rows, :], right())
            gb[r, member, to_z] = block.astype(BF16).reshape(NY, OWN, K)
            ry_start(r, q, member, j)
            if both_orders:

                @pl.when(i < NZ - 1)
                def _():
                    rz1_start(r, q, member, j)

            return 0

        lax.fori_loop(0, NZ, step, 0)

    def rs_other_order(r, q, member):
        for j in (4, 5, 3, 6, 2, 7, 1):
            rz1_start(r, q, member, j)

    def rs_mid_step(r, q, member, i):
        j = far_first(i)
        to_z = lax.rem(z + j, NZ)
        total = gb[r, member, to_z, y, 0:MAIN].astype(F32)
        arrived(ryin.at[r, member, j, pl.ds(1, NY - 1)], ry_r.at[q, member, j])
        for m in range(1, NY):
            total = total + ryin[r, member, j, m].astype(F32)
        szout[r, member, j] = total.astype(BF16)

        @pl.when(i < NZ - 1)
        def _():
            copy(
                szout.at[r, member, j], rz2in.at[r, member, j], rs_s.at[q, member], rz2_r.at[q, member], z_peer(j)
            ).start()

    def rs_mid_rest(r, q, member):
        total = gb[r, member, z, :, MAIN:OWN].astype(F32)
        arrived(rz1in.at[r, member, pl.ds(1, NZ - 1)], rz1_r.at[q, member])
        for j in range(1, NZ):
            total = total + rz1in[r, member, j].astype(F32)
        syout[r, member] = total.astype(BF16)
        for m in range(1, NY):
            to_y = lax.rem(y + m, NY)
            copy(
                syout.at[r, member, to_y], ry2in.at[r, member, m], rs_s.at[q, member], ry2_r.at[q, member], y_peer(m)
            ).start()

    def rs_mid(r, q, member):
        def step(i, _):
            rs_mid_step(r, q, member, i)
            return 0

        lax.fori_loop(0, NZ, step, 0)
        rs_mid_rest(r, q, member)

    def rs_end(r, q, member, out):
        total = syout[r, member, y].astype(F32)
        arrived(ry2in.at[r, member, pl.ds(1, NY - 1)], ry2_r.at[q, member])
        for m in range(1, NY):
            total = total + ry2in[r, member, m].astype(F32)
        out[member, MAIN:OWN] = total
        total = szout[r, member, 0].astype(F32)
        arrived(rz2in.at[r, member, pl.ds(1, NZ - 1)], rz2_r.at[q, member])
        for j in range(1, NZ):
            total = total + rz2in[r, member, j].astype(F32)
        out[member, 0:MAIN] = total
        sent(xt.at[0, pl.ds(0, SENT)], rs_s.at[q, member])

    def ayf_start(a, member, j):
        from_z = lax.rem(z - j + NZ, NZ)
        block = wb.at[a, member, from_z, y, pl.ds(0, MAIN)]
        for m in range(1, NY):
            copy(block, block, ag_s.at[member], ayf_r.at[member, j], y_peer(m)).start()

    def gather_start(a, member):
        wb[a, member, z, y] = wrow[member].astype(BF16)
        block = wb.at[a, member, z, y, pl.ds(MAIN, REST)]
        for m in range(1, NY):
            copy(block, block, ag_s.at[member], ay_r.at[member], y_peer(m)).start()
        block = wb.at[a, member, z, y, pl.ds(0, MAIN)]
        for j in (1, 7, 2, 6, 3, 5, 4):
            copy(block, block, ag_s.at[member], az_r.at[member, j], z_peer(j)).start()
        ayf_start(a, member, 0)

    def gather_forward(a, member):
        arrived(wb.at[a, member, z, pl.ds(0, NY - 1), pl.ds(0, REST)], ay_r.at[member])
        block = wb.at[a, member, z, :, pl.ds(MAIN, REST)]
        for j in (4, 5, 3, 6, 2, 7, 1):
            copy(block, block, ag_s.at[member], az2_r.at[member, j], z_peer(j)).start()

        def forward(i, _):
            j = far_first(NZ - 1 - i)
            arrived(wb.at[a, member, z, y, pl.ds(0, MAIN)], az_r.at[member, j])
            ayf_start(a, member, j)
            return 0

        lax.fori_loop(1, NZ, forward, 0)

    def gather_products(a, member):
        p[member] = jnp.zeros((ROWS, K), F32)

        def product(i, _):
            j = far_first(NZ - 1 - i)
            from_z = lax.rem(z - j + NZ, NZ)
            arrived(wb.at[a, member, z, pl.ds(0, NY - 1), pl.ds(0, MAIN)], ayf_r.at[member, j])

            @pl.when(i > 0)
            def _():
                arrived(wb.at[a, member, z, :, pl.ds(0, REST)], az2_r.at[member, j])

            product_of(a, member, from_z)
            return 0

        lax.fori_loop(0, NZ, product, 0)
        sent(xt.at[0, pl.ds(0, SENT)], ag_s.at[member])

    def product_of(a, member, from_z):
        cols = pl.ds(pl.multiple_of(from_z * BLOCK, BLOCK), BLOCK)
        p[member] += dot16(x_ref[member, :, cols], wb[a, member, from_z].reshape(BLOCK, K))

    def update(member):
        grad = (ga[member] - bm[member]) / SAMPLES
        wrow[member] = wrow[member] - STEP * (grad + RIDGE * wrow[member])

    wb[0] = w_ref[...].reshape(VIEWS, NZ, NY, OWN, K).astype(BF16)
    wrow[...] = w_ref[:, pl.ds(pl.multiple_of(s * OWN, OWN), OWN), :]
    p[...] = jnp.zeros_like(p)

    def first(i, _):
        cols = pl.ds(pl.multiple_of(i * BLOCK, BLOCK), BLOCK)
        for member in range(VIEWS):
            product_of(0, member, i)
            xt[member, cols, :] = x_ref[member, :, cols].T
        return 0

    lax.fori_loop(0, NZ, first, 0)
    pl.semaphore_wait(barrier, (NY - 1) + (NZ - 1) + (PEERS - 1))

    def outer(o, _):
        own_r, sum_r, next_r = 3 * o, 3 * o + 1, 3 * o + 2
        one, two = 2 * o + 1, 2 * o + 2
        vrs_start(o)
        for member in range(VIEWS):
            pb[member] = p[member].astype(BF16)
            rs_start(own_r, 0, member, lambda: pb[member])
        vrs_end(o)
        gram_v_end(o)
        vag_end(o)
        sb[...] = summed[o].astype(BF16)
        for member in range(VIEWS):
            rs_start(sum_r, 1, member, lambda: sb[...], both_orders=False)
        gram_y_end(o)
        for member in range(VIEWS):
            rs_mid(own_r, 0, member)
        for member in range(VIEWS):
            rs_other_order(sum_r, 1, member)
        gram_z_end(o)
        for member in range(VIEWS):
            rs_end(own_r, 0, member, ga)
        gram_end(o)
        both, scale = newton_init(o)

        def beside(i):
            for member in range(VIEWS):
                rs_mid_step(sum_r, 1, member, i)

        both = newton_turns(0, NZ, both, beside)
        for member in range(VIEWS):
            rs_mid_rest(sum_r, 1, member)
        both = newton_turns(NZ, NS_ITERS, both)
        white = both[:, K:] * jnp.sqrt(SAMPLES / scale)
        for member in range(VIEWS):
            rs_end(sum_r, 1, member, gs)
            bm[member] = dot32(gs[member], white)
            update(member)
            gather_start(one, member)
        for member in range(VIEWS):
            gather_forward(one, member)
        for member in range(VIEWS):
            gather_products(one, member)
            pb[member] = p[member].astype(BF16)
            rs_start(next_r, 0, member, lambda: pb[member])
        for member in range(VIEWS):
            rs_mid(next_r, 0, member)
        for member in range(VIEWS):
            rs_end(next_r, 0, member, ga)
            update(member)
            gather_start(two, member)
        for member in range(VIEWS):
            gather_forward(two, member)
        for member in range(VIEWS):
            gather_products(two, member)
        return 0

    lax.fori_loop(0, OUTER, outer, 0)
    vrs_start(OUTER)
    coeffs_ref[...] = wrow[...]
    vrs_end(OUTER)
    gram_v_end(OUTER)
    gram_y_end(OUTER)
    gram_z_end(OUTER)
    vag_end(OUTER)
    gram_end(OUTER)
    both, scale = newton_init(OUTER)
    both = newton_turns(0, NS_ITERS, both)
    scores_ref[...] = dot32(summed[OUTER], both[:, K:] * jnp.sqrt(SAMPLES / scale))


def body(view_data, init_coeffs):
    evals, reduces, gathers = OUTER + 1, 3 * OUTER, 2 * OUTER
    vmem, dma = pltpu.VMEM, pltpu.SemaphoreType.DMA
    scratch = [
        vmem((VIEWS, FEATS, ROWS), BF16),
        vmem((gathers + 1, VIEWS, NZ, NY, OWN, K), BF16),
        vmem((reduces, VIEWS, NZ, NY, OWN, K), BF16),
        vmem((VIEWS, ROWS, K), F32),
        vmem((VIEWS, ROWS, K), BF16),
        vmem((ROWS, K), BF16),
        vmem((VIEWS, OWN, K), F32),
        vmem((VIEWS, OWN, K), F32),
        vmem((VIEWS, OWN, K), F32),
        vmem((VIEWS, OWN, K), F32),
        vmem((evals, PEERS, SROWS, K), BF16),
        vmem((evals, PEERS, SROWS, K), BF16),
        vmem((evals, ROWS, K), F32),
        vmem((evals, K, K), F32),
        vmem((evals, PEERS, GROWS, K), F32),
        vmem((evals, PEERS, GROWS, K), F32),
        vmem((evals, GROWS, K), F32),
        vmem((evals, NY, GROWS, K), F32),
        vmem((evals, GROWS, K), F32),
        vmem((evals, NZ, GROWS, K), F32),
        vmem((reduces, VIEWS, NZ, NY, MAIN, K), BF16),
        vmem((reduces, VIEWS, NZ, MAIN, K), BF16),
        vmem((reduces, VIEWS, NZ, MAIN, K), BF16),
        vmem((reduces, VIEWS, NZ, NY, REST, K), BF16),
        vmem((reduces, VIEWS, NY, REST, K), BF16),
        vmem((reduces, VIEWS, NY, REST, K), BF16),
        *[dma((1,)) for _ in range(9)],
        dma((2, VIEWS, NZ)),
        dma((2, VIEWS)),
        dma((2, VIEWS)),
        dma((2, VIEWS)),
        dma((2, VIEWS)),
        dma((VIEWS, NZ)),
        dma((VIEWS, NZ)),
        dma((VIEWS,)),
        dma((VIEWS, NZ)),
        dma((VIEWS,)),
    ]
    return pl.pallas_call(
        kernel,
        out_shape=(jax.ShapeDtypeStruct((ROWS, K), F32), jax.ShapeDtypeStruct((VIEWS, OWN, K), F32)),
        in_specs=[pl.BlockSpec(memory_space=pltpu.VMEM)] * 2,
        out_specs=(pl.BlockSpec(memory_space=pltpu.VMEM),) * 2,
        scratch_shapes=scratch,
        compiler_params=pltpu.CompilerParams(collective_id=0, has_side_effects=True, vmem_limit_bytes=56 << 20),
        name="gcca",
    )(view_data, init_coeffs)


def solution(mesh):
    in_specs = (P("view", "samp", None), P("view", None, None))
    out_specs = (P("samp", None), P("view", "samp", None))
    return jax.shard_map(body, mesh=mesh, in_specs=in_specs, out_specs=out_specs, check_vma=False)
```

```python
import functools

import jax
import jax.numpy as jnp
from jax import lax
from jax.experimental import pallas as pl
from jax.experimental.pallas import tpu as pltpu
from jax.sharding import PartitionSpec as P

OUTER = 2
NS_ITERS = 12
RIDGE = 0.1
STEP = 0.5

HIGH = lax.Precision.HIGHEST
MESH = pl.DeviceIdType.MESH
F32 = jnp.float32
BF16 = jnp.bfloat16

NX, NC, NY, NZ = 4, 2, 4, 8
VIEWS, ROWS, FEATS, K = 2, 512, 2048, 128
BLOCK = FEATS // NZ
OWN = BLOCK // NY
MAIN, REST = 48, 16
SAMPLES = ROWS * NY * NZ
PEERS = NX * NC
SENT = (NY * NZ - 1) * OWN * K // ROWS
GROWS = K // (NX * NC)
SROWS = ROWS // (NX * NC)


def dot32(a, b):
    return jnp.dot(a, b, precision=HIGH, preferred_element_type=F32)


def dot16(a, b):
    return jnp.dot(a, b, preferred_element_type=F32)


def halves(a):
    hi = a.astype(BF16)
    return hi, (a - hi.astype(F32)).astype(BF16)


def far_first(i):
    odd = lax.rem(i, 2)
    return lax.rem(4 + odd * ((i + 1) // 2) - (1 - odd) * (i // 2), NZ)


def kernel(
    x_ref, w_ref, scores_ref, coeffs_ref,
    xt, wb, gb, p, pb, sb, wrow, bm, ga, gs,
    vloc, vin, summed, gram, gpart, gvin, gyout, gyin, gzout, gzin,
    ryin, szout, rz2in, rz1in, syout, ry2in,
    vrs_r, vag_r, gx_r, gy_r, gz_r, gv_r, vrs_s, vag_s, gram_s,
    ry_r, rz2_r, rz1_r, ry2_r, rs_s,
    az_r, ayf_r, ay_r, az2_r, ag_s,
):
    v = lax.axis_index("view")
    s = lax.axis_index("samp")
    y, z = lax.rem(s, NY), s // NY

    def y_peer(m):
        return {"view": v, "samp": z * NY + lax.rem(y + m, NY)}

    def z_peer(j):
        return {"view": v, "samp": lax.rem(z + j, NZ) * NY + y}

    def v_peer(j):
        return {"view": lax.rem(v + j, PEERS), "samp": s}

    def copy(src, dst, send, recv, device):
        return pltpu.make_async_remote_copy(
            src_ref=src, dst_ref=dst, send_sem=send, recv_sem=recv, device_id=device, device_id_type=MESH
        )

    def arrived(ref, recv):
        copy(ref, ref, ag_s.at[0], recv, y_peer(1)).wait_recv()

    def sent(ref, send):
        copy(ref, ref, send, ay_r.at[0], y_peer(1)).wait_send()

    barrier = pltpu.get_barrier_semaphore()
    for m in range(1, NY):
        pl.semaphore_signal(barrier, inc=1, device_id=y_peer(m), device_id_type=MESH)
    for j in range(1, NZ):
        pl.semaphore_signal(barrier, inc=1, device_id=z_peer(j), device_id_type=MESH)
    for j in range(1, PEERS):
        pl.semaphore_signal(barrier, inc=1, device_id=v_peer(j), device_id_type=MESH)

    def vrs_start(t):
        vloc[t] = (p[0] + p[1]).reshape(PEERS, SROWS, K).astype(vloc.dtype)
        for j in range(1, PEERS):
            to = lax.rem(v + j, PEERS)
            copy(vloc.at[t, to], vin.at[t, j], vrs_s.at[0], vrs_r.at[0], v_peer(j)).start()

    def vrs_end(t):
        total = vloc[t, v].astype(F32)
        arrived(vin.at[t, pl.ds(1, PEERS - 1)], vrs_r.at[0])
        for j in range(1, PEERS):
            total = total + vin[t, j].astype(F32)
        summed[t, pl.ds(v * SROWS, SROWS)] = total
        gpart[t] = dot32(total.T, total).reshape(PEERS, GROWS, K)
        for j in range(1, PEERS):
            to = lax.rem(v + j, PEERS)
            copy(gpart.at[t, to], gvin.at[t, j], gram_s.at[0], gx_r.at[0], v_peer(j)).start()
        block = summed.at[t, pl.ds(v * SROWS, SROWS)]
        for j in range(1, PEERS):
            copy(block, block, vag_s.at[0], vag_r.at[0], v_peer(j)).start()

    def vag_end(t):
        arrived(summed.at[t, pl.ds(0, ROWS - SROWS)], vag_r.at[0])

    def gram_v_end(t):
        total = gpart[t, v]
        arrived(gvin.at[t, pl.ds(1, PEERS - 1)], gx_r.at[0])
        for j in range(1, PEERS):
            total = total + gvin[t, j]
        gyout[t] = total
        for m in range(1, NY):
            copy(gyout.at[t], gyin.at[t, m], gram_s.at[0], gy_r.at[0], y_peer(m)).start()

    def gram_y_end(t):
        total = gyout[t]
        arrived(gyin.at[t, pl.ds(1, NY - 1)], gy_r.at[0])
        for m in range(1, NY):
            total = total + gyin[t, m]
        gzout[t] = total
        for j in (4, 5, 3, 6, 2, 7, 1):
            copy(gzout.at[t], gzin.at[t, j], gram_s.at[0], gz_r.at[0], z_peer(j)).start()

    def gram_z_end(t):
        total = gzout[t]
        arrived(gzin.at[t, pl.ds(1, NZ - 1)], gz_r.at[0])
        for j in range(1, NZ):
            total = total + gzin[t, j]
        gram[t, pl.ds(v * GROWS, GROWS)] = total
        block = gram.at[t, pl.ds(v * GROWS, GROWS)]
        for j in range(1, PEERS):
            copy(block, block, gram_s.at[0], gv_r.at[0], v_peer(j)).start()

    def gram_end(t):
        arrived(gram.at[t, pl.ds(0, K - GROWS)], gv_r.at[0])
        sent(vin.at[t, pl.ds(1, PEERS - 1)], vrs_s.at[0])
        sent(summed.at[t, pl.ds(0, ROWS - SROWS)], vag_s.at[0])
        sent(summed.at[t, pl.ds(0, (3 * 7 + 3) * GROWS)], gram_s.at[0])

    def eye_mat():
        row = lax.broadcasted_iota(jnp.int32, (K, K), 0)
        col = lax.broadcasted_iota(jnp.int32, (K, K), 1)
        return jnp.where(row == col, 1.0, 0.0).astype(F32)

    def newton_init(t):
        eye = eye_mat()
        full = gram[t]
        trace = jnp.sum(full * eye, keepdims=True)
        shrunk = full + trace / K * eye
        scale = jnp.sqrt(jnp.sum(shrunk * shrunk, keepdims=True))
        return jnp.concatenate([shrunk / scale, eye], axis=1), scale

    def newton_turns(first, last, both, beside=None):
        eye = eye_mat()

        def turn(i, both):
            approx, inverse = both[:, :K], both[:, K:]
            hi, lo = halves(both)
            ah, al, ih, il = hi[:, :K], lo[:, :K], hi[:, K:], lo[:, K:]
            none = jnp.zeros((K, K), BF16)
            left = jnp.concatenate([ih, il], axis=1)
            right = jnp.concatenate([jnp.concatenate([ah, al], axis=1), jnp.concatenate([ah, none], axis=1)], axis=0)
            parts = dot16(left, right)
            factor = 0.5 * (3.0 * eye - (parts[:, :K] + parts[:, K:]))
            fh, fl = halves(factor)
            both = dot16(jnp.concatenate([fh, fl], axis=1), jnp.concatenate([hi, hi], axis=0)) + dot16(fh, lo)
            if beside is not None:
                beside(i)
            return both

        return lax.fori_loop(first, last, turn, both)

    def ry_start(r, q, member, j):
        to_z = lax.rem(z + j, NZ)
        for m in range(1, NY):
            to_y = lax.rem(y + m, NY)
            copy(
                gb.at[r, member, to_z, to_y, pl.ds(0, MAIN)], ryin.at[r, member, j, m],
                rs_s.at[q, member], ry_r.at[q, member, j], y_peer(m),
            ).start()

    def rz1_start(r, q, member, j):
        to_z = lax.rem(z + j, NZ)
        copy(
            gb.at[r, member, to_z, :, pl.ds(MAIN, REST)], rz1in.at[r, member, j],
            rs_s.at[q, member], rz1_r.at[q, member], z_peer(j),
        ).start()

    def rs_start(r, q, member, right, both_orders=True):
        def step(i, _):
            j = far_first(i)
            to_z = lax.rem(z + j, NZ)
            rows = pl.ds(pl.multiple_of(to_z * BLOCK, BLOCK), BLOCK)
            block = dot16(xt[member, rows, :], right())
            gb[r, member, to_z] = block.astype(BF16).reshape(NY, OWN, K)
            ry_start(r, q, member, j)
            if both_orders:

                @pl.when(i < NZ - 1)
                def _():
                    rz1_start(r, q, member, j)

            return 0

        lax.fori_loop(0, NZ, step, 0)

    def rs_other_order(r, q, member):
        for j in (4, 5, 3, 6, 2, 7, 1):
            rz1_start(r, q, member, j)

    def rs_mid_step(r, q, member, i):
        j = far_first(i)
        to_z = lax.rem(z + j, NZ)
        total = gb[r, member, to_z, y, 0:MAIN].astype(F32)
        arrived(ryin.at[r, member, j, pl.ds(1, NY - 1)], ry_r.at[q, member, j])
        for m in range(1, NY):
            total = total + ryin[r, member, j, m].astype(F32)
        szout[r, member, j] = total.astype(BF16)

        @pl.when(i < NZ - 1)
        def _():
            copy(
                szout.at[r, member, j], rz2in.at[r, member, j], rs_s.at[q, member], rz2_r.at[q, member], z_peer(j)
            ).start()

    def rs_mid_rest(r, q, member):
        total = gb[r, member, z, :, MAIN:OWN].astype(F32)
        arrived(rz1in.at[r, member, pl.ds(1, NZ - 1)], rz1_r.at[q, member])
        for j in range(1, NZ):
            total = total + rz1in[r, member, j].astype(F32)
        syout[r, member] = total.astype(BF16)
        for m in range(1, NY):
            to_y = lax.rem(y + m, NY)
            copy(
                syout.at[r, member, to_y], ry2in.at[r, member, m], rs_s.at[q, member], ry2_r.at[q, member], y_peer(m)
            ).start()

    def rs_mid(r, q, member):
        def step(i, _):
            rs_mid_step(r, q, member, i)
            return 0

        lax.fori_loop(0, NZ, step, 0)
        rs_mid_rest(r, q, member)

    def rs_end(r, q, member, out):
        total = syout[r, member, y].astype(F32)
        arrived(ry2in.at[r, member, pl.ds(1, NY - 1)], ry2_r.at[q, member])
        for m in range(1, NY):
            total = total + ry2in[r, member, m].astype(F32)
        out[member, MAIN:OWN] = total
        total = szout[r, member, 0].astype(F32)
        arrived(rz2in.at[r, member, pl.ds(1, NZ - 1)], rz2_r.at[q, member])
        for j in range(1, NZ):
            total = total + rz2in[r, member, j].astype(F32)
        out[member, 0:MAIN] = total
        sent(xt.at[0, pl.ds(0, SENT)], rs_s.at[q, member])

    def ayf_start(a, member, j):
        from_z = lax.rem(z - j + NZ, NZ)
        block = wb.at[a, member, from_z, y, pl.ds(0, MAIN)]
        for m in range(1, NY):
            copy(block, block, ag_s.at[member], ayf_r.at[member, j], y_peer(m)).start()

    def gather_start(a, member):
        wb[a, member, z, y] = wrow[member].astype(BF16)
        block = wb.at[a, member, z, y, pl.ds(MAIN, REST)]
        for m in range(1, NY):
            copy(block, block, ag_s.at[member], ay_r.at[member], y_peer(m)).start()
        block = wb.at[a, member, z, y, pl.ds(0, MAIN)]
        for j in (1, 7, 2, 6, 3, 5, 4):
            copy(block, block, ag_s.at[member], az_r.at[member, j], z_peer(j)).start()
        ayf_start(a, member, 0)

    def gather_forward(a, member):
        arrived(wb.at[a, member, z, pl.ds(0, NY - 1), pl.ds(0, REST)], ay_r.at[member])
        block = wb.at[a, member, z, :, pl.ds(MAIN, REST)]
        for j in (4, 5, 3, 6, 2, 7, 1):
            copy(block, block, ag_s.at[member], az2_r.at[member, j], z_peer(j)).start()

        def forward(i, _):
            j = far_first(NZ - 1 - i)
            arrived(wb.at[a, member, z, y, pl.ds(0, MAIN)], az_r.at[member, j])
            ayf_start(a, member, j)
            return 0

        lax.fori_loop(1, NZ, forward, 0)

    def gather_products(a, member):
        p[member] = jnp.zeros((ROWS, K), F32)

        def product(i, _):
            j = far_first(NZ - 1 - i)
            from_z = lax.rem(z - j + NZ, NZ)
            arrived(wb.at[a, member, z, pl.ds(0, NY - 1), pl.ds(0, MAIN)], ayf_r.at[member, j])

            @pl.when(i > 0)
            def _():
                arrived(wb.at[a, member, z, :, pl.ds(0, REST)], az2_r.at[member, j])

            product_of(a, member, from_z)
            return 0

        lax.fori_loop(0, NZ, product, 0)
        sent(xt.at[0, pl.ds(0, SENT)], ag_s.at[member])

    def product_of(a, member, from_z):
        cols = pl.ds(pl.multiple_of(from_z * BLOCK, BLOCK), BLOCK)
        p[member] += dot16(x_ref[member, :, cols], wb[a, member, from_z].reshape(BLOCK, K))

    def update(member):
        grad = (ga[member] - bm[member]) / SAMPLES
        wrow[member] = wrow[member] - STEP * (grad + RIDGE * wrow[member])

    wb[0] = w_ref[...].reshape(VIEWS, NZ, NY, OWN, K).astype(BF16)
    wrow[...] = w_ref[:, pl.ds(pl.multiple_of(s * OWN, OWN), OWN), :]
    p[...] = jnp.zeros_like(p)

    def first(i, _):
        cols = pl.ds(pl.multiple_of(i * BLOCK, BLOCK), BLOCK)
        for member in range(VIEWS):
            product_of(0, member, i)
            xt[member, cols, :] = x_ref[member, :, cols].T
        return 0

    lax.fori_loop(0, NZ, first, 0)
    pl.semaphore_wait(barrier, (NY - 1) + (NZ - 1) + (PEERS - 1))

    def outer(o, _):
        own_r, sum_r, next_r = 3 * o, 3 * o + 1, 3 * o + 2
        one, two = 2 * o + 1, 2 * o + 2
        vrs_start(o)
        for member in range(VIEWS):
            pb[member] = p[member].astype(BF16)
            rs_start(own_r, 0, member, lambda: pb[member])
        vrs_end(o)
        rs_mid(own_r, 0, 0)
        gram_v_end(o)
        rs_mid(own_r, 0, 1)
        vag_end(o)
        sb[...] = summed[o].astype(BF16)
        rs_start(sum_r, 1, 0, lambda: sb[...], both_orders=False)
        gram_y_end(o)
        rs_other_order(sum_r, 1, 0)
        rs_start(sum_r, 1, 1, lambda: sb[...], both_orders=False)
        rs_other_order(sum_r, 1, 1)
        gram_z_end(o)
        rs_end(own_r, 0, 0, ga)
        rs_end(own_r, 0, 1, ga)
        rs_mid(sum_r, 1, 0)
        gram_end(o)
        both, scale = newton_init(o)
        both = newton_turns(0, NZ, both, lambda i: rs_mid_step(sum_r, 1, 1, i))
        rs_mid_rest(sum_r, 1, 1)
        both = newton_turns(NZ, NS_ITERS, both)
        white = both[:, K:] * jnp.sqrt(SAMPLES / scale)
        for member in range(VIEWS):
            rs_end(sum_r, 1, member, gs)
            bm[member] = dot32(gs[member], white)
            update(member)
            gather_start(one, member)
        for member in range(VIEWS):
            gather_forward(one, member)
        for member in range(VIEWS):
            gather_products(one, member)
            pb[member] = p[member].astype(BF16)
            rs_start(next_r, 0, member, lambda: pb[member])
        for member in range(VIEWS):
            rs_mid(next_r, 0, member)
        for member in range(VIEWS):
            rs_end(next_r, 0, member, ga)
            update(member)
            gather_start(two, member)
        for member in range(VIEWS):
            gather_forward(two, member)
        for member in range(VIEWS):
            gather_products(two, member)
        return 0

    lax.fori_loop(0, OUTER, outer, 0)
    vrs_start(OUTER)
    coeffs_ref[...] = wrow[...]
    vrs_end(OUTER)
    gram_v_end(OUTER)
    gram_y_end(OUTER)
    gram_z_end(OUTER)
    vag_end(OUTER)
    gram_end(OUTER)
    both, scale = newton_init(OUTER)
    both = newton_turns(0, NS_ITERS, both)
    scores_ref[...] = dot32(summed[OUTER], both[:, K:] * jnp.sqrt(SAMPLES / scale))


def keep(scores_ref, coeffs_ref, scores_out, coeffs_out):
    scores_out[...] = scores_ref[...]
    coeffs_out[...] = coeffs_ref[...]


def body(view_data, init_coeffs):
    evals, reduces, gathers = OUTER + 1, 3 * OUTER, 2 * OUTER
    vmem, dma = pltpu.VMEM, pltpu.SemaphoreType.DMA
    scratch = [
        vmem((VIEWS, FEATS, ROWS), BF16),
        vmem((gathers + 1, VIEWS, NZ, NY, OWN, K), BF16),
        vmem((reduces, VIEWS, NZ, NY, OWN, K), BF16),
        vmem((VIEWS, ROWS, K), F32),
        vmem((VIEWS, ROWS, K), BF16),
        vmem((ROWS, K), BF16),
        vmem((VIEWS, OWN, K), F32),
        vmem((VIEWS, OWN, K), F32),
        vmem((VIEWS, OWN, K), F32),
        vmem((VIEWS, OWN, K), F32),
        vmem((evals, PEERS, SROWS, K), BF16),
        vmem((evals, PEERS, SROWS, K), BF16),
        vmem((evals, ROWS, K), F32),
        vmem((evals, K, K), F32),
        vmem((evals, PEERS, GROWS, K), F32),
        vmem((evals, PEERS, GROWS, K), F32),
        vmem((evals, GROWS, K), F32),
        vmem((evals, NY, GROWS, K), F32),
        vmem((evals, GROWS, K), F32),
        vmem((evals, NZ, GROWS, K), F32),
        vmem((reduces, VIEWS, NZ, NY, MAIN, K), BF16),
        vmem((reduces, VIEWS, NZ, MAIN, K), BF16),
        vmem((reduces, VIEWS, NZ, MAIN, K), BF16),
        vmem((reduces, VIEWS, NZ, NY, REST, K), BF16),
        vmem((reduces, VIEWS, NY, REST, K), BF16),
        vmem((reduces, VIEWS, NY, REST, K), BF16),
        *[dma((1,)) for _ in range(9)],
        dma((2, VIEWS, NZ)),
        dma((2, VIEWS)),
        dma((2, VIEWS)),
        dma((2, VIEWS)),
        dma((2, VIEWS)),
        dma((VIEWS, NZ)),
        dma((VIEWS, NZ)),
        dma((VIEWS,)),
        dma((VIEWS, NZ)),
        dma((VIEWS,)),
    ]
    results = pl.pallas_call(
        kernel,
        out_shape=(jax.ShapeDtypeStruct((ROWS, K), F32), jax.ShapeDtypeStruct((VIEWS, OWN, K), F32)),
        in_specs=[pl.BlockSpec(memory_space=pltpu.VMEM)] * 2,
        out_specs=(pl.BlockSpec(memory_space=pltpu.VMEM),) * 2,
        scratch_shapes=scratch,
        compiler_params=pltpu.CompilerParams(collective_id=0, has_side_effects=True, vmem_limit_bytes=56 << 20),
        name="gcca",
    )(view_data, init_coeffs)
    return pl.pallas_call(
        keep,
        out_shape=(jax.ShapeDtypeStruct((ROWS, K), F32), jax.ShapeDtypeStruct((VIEWS, OWN, K), F32)),
        in_specs=[pl.BlockSpec(memory_space=pltpu.VMEM)] * 2,
        out_specs=(pl.BlockSpec(memory_space=pltpu.VMEM),) * 2,
        name="keep",
    )(*results)


def solution(mesh):
    in_specs = (P("view", "samp", None), P("view", None, None))
    out_specs = (P("samp", None), P("view", "samp", None))
    return jax.shard_map(body, mesh=mesh, in_specs=in_specs, out_specs=out_specs, check_vma=False)
```

```python
import functools

import jax
import jax.numpy as jnp
from jax import lax
from jax.experimental import pallas as pl
from jax.experimental.pallas import tpu as pltpu
from jax.sharding import PartitionSpec as P

OUTER = 2
NS_ITERS = 12
RIDGE = 0.1
STEP = 0.5

HIGH = lax.Precision.HIGHEST
MESH = pl.DeviceIdType.MESH
F32 = jnp.float32
BF16 = jnp.bfloat16

NX, NC, NY, NZ = 4, 2, 4, 8
VIEWS, ROWS, FEATS, K = 2, 512, 2048, 128
BLOCK = FEATS // NZ
OWN = BLOCK // NY
MAIN, REST = 48, 16
SAMPLES = ROWS * NY * NZ
PEERS = NX * NC
SENT = (NY * NZ - 1) * OWN * K // ROWS
GROWS = K // (NX * NC)
HALF = ROWS // NC


def dot32(a, b):
    return jnp.dot(a, b, precision=HIGH, preferred_element_type=F32)


def dot16(a, b):
    return jnp.dot(a, b, preferred_element_type=F32)


def halves(a):
    hi = a.astype(BF16)
    return hi, (a - hi.astype(F32)).astype(BF16)


def far_first(i):
    odd = lax.rem(i, 2)
    return lax.rem(4 + odd * ((i + 1) // 2) - (1 - odd) * (i // 2), NZ)


def kernel(
    x_ref, w_ref, scores_ref, coeffs_ref,
    xt, wb, gb, p, pb, sb, wrow, bm, ga, gs,
    cout, cin, xin, summed, gram, gpart, gvin, gyout, gyin, gzout, gzin,
    ryin, szout, rz2in, rz1in, syout, ry2in,
    core_r, core_s, vrs_r, vag_r, gx_r, gy_r, gz_r, gv_r, vrs_s, vag_s, gram_s,
    ry_r, rz2_r, rz1_r, ry2_r, rs_s,
    az_r, ayf_r, ay_r, az2_r, ag_s,
):
    v = lax.axis_index("view")
    s = lax.axis_index("samp")
    x, core = v // NC, lax.rem(v, NC)
    y, z = lax.rem(s, NY), s // NY
    sibling = {"view": v + 1 - 2 * core, "samp": s}

    def y_peer(m):
        return {"view": v, "samp": z * NY + lax.rem(y + m, NY)}

    def z_peer(j):
        return {"view": v, "samp": lax.rem(z + j, NZ) * NY + y}

    def v_peer(j):
        return {"view": lax.rem(v + j, PEERS), "samp": s}

    def copy(src, dst, send, recv, device):
        return pltpu.make_async_remote_copy(
            src_ref=src, dst_ref=dst, send_sem=send, recv_sem=recv, device_id=device, device_id_type=MESH
        )

    def arrived(ref, recv):
        copy(ref, ref, ag_s.at[0], recv, y_peer(1)).wait_recv()

    def sent(ref, send):
        copy(ref, ref, send, ay_r.at[0], y_peer(1)).wait_send()

    barrier = pltpu.get_barrier_semaphore()
    for m in range(1, NY):
        pl.semaphore_signal(barrier, inc=1, device_id=y_peer(m), device_id_type=MESH)
    for j in range(1, NZ):
        pl.semaphore_signal(barrier, inc=1, device_id=z_peer(j), device_id_type=MESH)
    for j in range(1, PEERS):
        pl.semaphore_signal(barrier, inc=1, device_id=v_peer(j), device_id_type=MESH)

    def vrs_start(t):
        away = pl.ds(pl.multiple_of((1 - core) * HALF, HALF), HALF)
        cout[t] = p[0, away] + p[1, away]
        copy(cout.at[t], cin.at[t], core_s.at[0], core_r.at[0], sibling).start()

    def vrs_mid(t):
        here = pl.ds(pl.multiple_of(core * HALF, HALF), HALF)
        total = p[0, here] + p[1, here]
        arrived(cin.at[t], core_r.at[0])
        xin[t, x] = (total + cin[t]).astype(BF16)
        for k in (2, 1, 3):
            copy(xin.at[t, x], xin.at[t, x], vrs_s.at[0], vrs_r.at[0], v_peer(2 * k)).start()

    def vrs_end(t):
        here = pl.ds(pl.multiple_of(core * HALF, HALF), HALF)
        arrived(xin.at[t, pl.ds(0, NX - 1)], vrs_r.at[0])
        total = xin[t, 0].astype(F32)
        for k in range(1, NX):
            total = total + xin[t, k].astype(F32)
        summed[t, here] = total
        gpart[t] = dot32(total.T, total).reshape(PEERS, GROWS, K)
        copy(gpart.at[t, v + 1 - 2 * core], gvin.at[t], gram_s.at[0], gx_r.at[0], sibling).start()
        copy(summed.at[t, here], summed.at[t, here], vag_s.at[0], vag_r.at[0], sibling).start()

    def vag_end(t):
        arrived(summed.at[t, pl.ds(0, HALF)], vag_r.at[0])

    def gram_v_end(t):
        arrived(gvin.at[t], gx_r.at[0])
        gyout[t] = gpart[t, v] + gvin[t]
        for m in range(1, NY):
            copy(gyout.at[t], gyin.at[t, m], gram_s.at[0], gy_r.at[0], y_peer(m)).start()

    def gram_y_end(t):
        total = gyout[t]
        arrived(gyin.at[t, pl.ds(1, NY - 1)], gy_r.at[0])
        for m in range(1, NY):
            total = total + gyin[t, m]
        gzout[t] = total
        for j in (4, 5, 3, 6, 2, 7, 1):
            copy(gzout.at[t], gzin.at[t, j], gram_s.at[0], gz_r.at[0], z_peer(j)).start()

    def gram_z_end(t):
        total = gzout[t]
        arrived(gzin.at[t, pl.ds(1, NZ - 1)], gz_r.at[0])
        for j in range(1, NZ):
            total = total + gzin[t, j]
        gram[t, pl.ds(v * GROWS, GROWS)] = total
        block = gram.at[t, pl.ds(v * GROWS, GROWS)]
        for j in range(1, PEERS):
            copy(block, block, gram_s.at[0], gv_r.at[0], v_peer(j)).start()

    def gram_end(t):
        arrived(gram.at[t, pl.ds(0, K - GROWS)], gv_r.at[0])
        sent(cout.at[t], core_s.at[0])
        sent(xin.at[t, pl.ds(0, NX - 1)], vrs_s.at[0])
        sent(summed.at[t, pl.ds(0, HALF)], vag_s.at[0])
        sent(summed.at[t, pl.ds(0, (NY + NZ + PEERS - 2) * GROWS)], gram_s.at[0])

    def eye_mat():
        row = lax.broadcasted_iota(jnp.int32, (K, K), 0)
        col = lax.broadcasted_iota(jnp.int32, (K, K), 1)
        return jnp.where(row == col, 1.0, 0.0).astype(F32)

    def newton_init(t):
        eye = eye_mat()
        full = gram[t]
        trace = jnp.sum(full * eye, keepdims=True)
        shrunk = full + trace / K * eye
        scale = jnp.sqrt(jnp.sum(shrunk * shrunk, keepdims=True))
        return jnp.concatenate([shrunk / scale, eye], axis=1), scale

    def newton_turns(first, last, both, beside=None):
        eye = eye_mat()

        def turn(i, both):
            approx, inverse = both[:, :K], both[:, K:]
            hi, lo = halves(both)
            ah, al, ih, il = hi[:, :K], lo[:, :K], hi[:, K:], lo[:, K:]
            none = jnp.zeros((K, K), BF16)
            left = jnp.concatenate([ih, il], axis=1)
            right = jnp.concatenate([jnp.concatenate([ah, al], axis=1), jnp.concatenate([ah, none], axis=1)], axis=0)
            parts = dot16(left, right)
            factor = 0.5 * (3.0 * eye - (parts[:, :K] + parts[:, K:]))
            fh, fl = halves(factor)
            both = dot16(jnp.concatenate([fh, fl], axis=1), jnp.concatenate([hi, hi], axis=0)) + dot16(fh, lo)
            if beside is not None:
                beside(i)
            return both

        return lax.fori_loop(first, last, turn, both)

    def ry_start(r, q, member, j):
        to_z = lax.rem(z + j, NZ)
        for m in range(1, NY):
            to_y = lax.rem(y + m, NY)
            copy(
                gb.at[r, member, to_z, to_y, pl.ds(0, MAIN)], ryin.at[r, member, j, m],
                rs_s.at[q, member], ry_r.at[q, member, j], y_peer(m),
            ).start()

    def rz1_start(r, q, member, j):
        to_z = lax.rem(z + j, NZ)
        copy(
            gb.at[r, member, to_z, :, pl.ds(MAIN, REST)], rz1in.at[r, member, j],
            rs_s.at[q, member], rz1_r.at[q, member], z_peer(j),
        ).start()

    def rs_start(r, q, member, right, both_orders=True):
        def step(i, _):
            j = far_first(i)
            to_z = lax.rem(z + j, NZ)
            rows = pl.ds(pl.multiple_of(to_z * BLOCK, BLOCK), BLOCK)
            block = dot16(xt[member, rows, :], right())
            gb[r, member, to_z] = block.astype(BF16).reshape(NY, OWN, K)
            ry_start(r, q, member, j)
            if both_orders:

                @pl.when(i < NZ - 1)
                def _():
                    rz1_start(r, q, member, j)

            return 0

        lax.fori_loop(0, NZ, step, 0)

    def rs_other_order(r, q, member):
        for j in (4, 5, 3, 6, 2, 7, 1):
            rz1_start(r, q, member, j)

    def rs_mid_step(r, q, member, i):
        j = far_first(i)
        to_z = lax.rem(z + j, NZ)
        total = gb[r, member, to_z, y, 0:MAIN].astype(F32)
        arrived(ryin.at[r, member, j, pl.ds(1, NY - 1)], ry_r.at[q, member, j])
        for m in range(1, NY):
            total = total + ryin[r, member, j, m].astype(F32)
        szout[r, member, j] = total.astype(BF16)

        @pl.when(i < NZ - 1)
        def _():
            copy(
                szout.at[r, member, j], rz2in.at[r, member, j], rs_s.at[q, member], rz2_r.at[q, member], z_peer(j)
            ).start()

    def rs_mid_rest(r, q, member):
        total = gb[r, member, z, :, MAIN:OWN].astype(F32)
        arrived(rz1in.at[r, member, pl.ds(1, NZ - 1)], rz1_r.at[q, member])
        for j in range(1, NZ):
            total = total + rz1in[r, member, j].astype(F32)
        syout[r, member] = total.astype(BF16)
        for m in range(1, NY):
            to_y = lax.rem(y + m, NY)
            copy(
                syout.at[r, member, to_y], ry2in.at[r, member, m], rs_s.at[q, member], ry2_r.at[q, member], y_peer(m)
            ).start()

    def rs_mid(r, q, member):
        def step(i, _):
            rs_mid_step(r, q, member, i)
            return 0

        lax.fori_loop(0, NZ, step, 0)
        rs_mid_rest(r, q, member)

    def rs_end(r, q, member, out):
        total = syout[r, member, y].astype(F32)
        arrived(ry2in.at[r, member, pl.ds(1, NY - 1)], ry2_r.at[q, member])
        for m in range(1, NY):
            total = total + ry2in[r, member, m].astype(F32)
        out[member, MAIN:OWN] = total
        total = szout[r, member, 0].astype(F32)
        arrived(rz2in.at[r, member, pl.ds(1, NZ - 1)], rz2_r.at[q, member])
        for j in range(1, NZ):
            total = total + rz2in[r, member, j].astype(F32)
        out[member, 0:MAIN] = total
        sent(xt.at[0, pl.ds(0, SENT)], rs_s.at[q, member])

    def ayf_start(a, member, j):
        from_z = lax.rem(z - j + NZ, NZ)
        block = wb.at[a, member, from_z, y, pl.ds(0, MAIN)]
        for m in range(1, NY):
            copy(block, block, ag_s.at[member], ayf_r.at[member, j], y_peer(m)).start()

    def gather_start(a, member):
        wb[a, member, z, y] = wrow[member].astype(BF16)
        block = wb.at[a, member, z, y, pl.ds(MAIN, REST)]
        for m in range(1, NY):
            copy(block, block, ag_s.at[member], ay_r.at[member], y_peer(m)).start()
        ayf_start(a, member, 0)
        block = wb.at[a, member, z, y, pl.ds(0, MAIN)]
        for j in (1, 7, 2, 6, 3, 5, 4):
            copy(block, block, ag_s.at[member], az_r.at[member, j], z_peer(j)).start()

    def gather_forward(a, member):
        arrived(wb.at[a, member, z, pl.ds(0, NY - 1), pl.ds(0, REST)], ay_r.at[member])
        block = wb.at[a, member, z, :, pl.ds(MAIN, REST)]
        for j in (1, 7, 2, 6, 3, 5, 4):
            copy(block, block, ag_s.at[member], az2_r.at[member, j], z_peer(j)).start()

        def forward(i, _):
            j = far_first(NZ - 1 - i)
            arrived(wb.at[a, member, z, y, pl.ds(0, MAIN)], az_r.at[member, j])
            ayf_start(a, member, j)
            return 0

        lax.fori_loop(1, NZ, forward, 0)

    def gather_products(a, member):
        p[member] = jnp.zeros((ROWS, K), F32)

        def product(i, _):
            j = far_first(NZ - 1 - i)
            from_z = lax.rem(z - j + NZ, NZ)
            arrived(wb.at[a, member, z, pl.ds(0, NY - 1), pl.ds(0, MAIN)], ayf_r.at[member, j])

            @pl.when(i > 0)
            def _():
                arrived(wb.at[a, member, z, :, pl.ds(0, REST)], az2_r.at[member, j])

            product_of(a, member, from_z)
            return 0

        lax.fori_loop(0, NZ, product, 0)
        sent(xt.at[0, pl.ds(0, SENT)], ag_s.at[member])

    def product_of(a, member, from_z):
        cols = pl.ds(pl.multiple_of(from_z * BLOCK, BLOCK), BLOCK)
        p[member] += dot16(x_ref[member, :, cols], wb[a, member, from_z].reshape(BLOCK, K))

    def update(member):
        grad = (ga[member] - bm[member]) / SAMPLES
        wrow[member] = wrow[member] - STEP * (grad + RIDGE * wrow[member])

    wb[0] = w_ref[...].reshape(VIEWS, NZ, NY, OWN, K).astype(BF16)
    wrow[...] = w_ref[:, pl.ds(pl.multiple_of(s * OWN, OWN), OWN), :]
    p[...] = jnp.zeros_like(p)

    def first(i, _):
        cols = pl.ds(pl.multiple_of(i * BLOCK, BLOCK), BLOCK)
        for member in range(VIEWS):
            product_of(0, member, i)
            xt[member, cols, :] = x_ref[member, :, cols].T
        return 0

    lax.fori_loop(0, NZ, first, 0)
    pl.semaphore_wait(barrier, (NY - 1) + (NZ - 1) + (PEERS - 1))

    def outer(o, _):
        own_r, sum_r, next_r = 3 * o, 3 * o + 1, 3 * o + 2
        one, two = 2 * o + 1, 2 * o + 2
        vrs_start(o)
        pb[0] = p[0].astype(BF16)
        rs_start(own_r, 0, 0, lambda: pb[0])
        vrs_mid(o)
        pb[1] = p[1].astype(BF16)
        rs_start(own_r, 0, 1, lambda: pb[1])
        vrs_end(o)
        gram_v_end(o)
        rs_mid(own_r, 0, 0)
        vag_end(o)
        sb[...] = summed[o].astype(BF16)
        rs_start(sum_r, 1, 0, lambda: sb[...], both_orders=False)
        gram_y_end(o)
        rs_mid(own_r, 0, 1)
        rs_other_order(sum_r, 1, 0)
        rs_start(sum_r, 1, 1, lambda: sb[...], both_orders=False)
        rs_other_order(sum_r, 1, 1)
        gram_z_end(o)
        rs_end(own_r, 0, 0, ga)
        rs_end(own_r, 0, 1, ga)
        rs_mid(sum_r, 1, 0)
        gram_end(o)
        both, scale = newton_init(o)
        both = newton_turns(0, NZ, both, lambda i: rs_mid_step(sum_r, 1, 1, i))
        rs_mid_rest(sum_r, 1, 1)
        both = newton_turns(NZ, NS_ITERS, both)
        white = both[:, K:] * jnp.sqrt(SAMPLES / scale)
        for member in range(VIEWS):
            rs_end(sum_r, 1, member, gs)
            bm[member] = dot32(gs[member], white)
            update(member)
            gather_start(one, member)
        for member in range(VIEWS):
            gather_forward(one, member)
        for member in range(VIEWS):
            gather_products(one, member)
            pb[member] = p[member].astype(BF16)
            rs_start(next_r, 0, member, lambda: pb[member])
        for member in range(VIEWS):
            rs_mid(next_r, 0, member)
        for member in range(VIEWS):
            rs_end(next_r, 0, member, ga)
            update(member)
            gather_start(two, member)
        for member in range(VIEWS):
            gather_forward(two, member)
        for member in range(VIEWS):
            gather_products(two, member)
        return 0

    lax.fori_loop(0, OUTER, outer, 0)
    vrs_start(OUTER)
    coeffs_ref[...] = wrow[...]
    vrs_mid(OUTER)
    vrs_end(OUTER)
    gram_v_end(OUTER)
    gram_y_end(OUTER)
    gram_z_end(OUTER)
    vag_end(OUTER)
    gram_end(OUTER)
    both, scale = newton_init(OUTER)
    both = newton_turns(0, NS_ITERS, both)
    scores_ref[...] = dot32(summed[OUTER], both[:, K:] * jnp.sqrt(SAMPLES / scale))


def keep(scores_ref, coeffs_ref, scores_out, coeffs_out):
    scores_out[...] = scores_ref[...]
    coeffs_out[...] = coeffs_ref[...]


def body(view_data, init_coeffs):
    evals, reduces, gathers = OUTER + 1, 3 * OUTER, 2 * OUTER
    vmem, dma = pltpu.VMEM, pltpu.SemaphoreType.DMA
    scratch = [
        vmem((VIEWS, FEATS, ROWS), BF16),
        vmem((gathers + 1, VIEWS, NZ, NY, OWN, K), BF16),
        vmem((reduces, VIEWS, NZ, NY, OWN, K), BF16),
        vmem((VIEWS, ROWS, K), F32),
        vmem((VIEWS, ROWS, K), BF16),
        vmem((ROWS, K), BF16),
        vmem((VIEWS, OWN, K), F32),
        vmem((VIEWS, OWN, K), F32),
        vmem((VIEWS, OWN, K), F32),
        vmem((VIEWS, OWN, K), F32),
        vmem((evals, HALF, K), F32),
        vmem((evals, HALF, K), F32),
        vmem((evals, NX, HALF, K), BF16),
        vmem((evals, ROWS, K), F32),
        vmem((evals, K, K), F32),
        vmem((evals, PEERS, GROWS, K), F32),
        vmem((evals, GROWS, K), F32),
        vmem((evals, GROWS, K), F32),
        vmem((evals, NY, GROWS, K), F32),
        vmem((evals, GROWS, K), F32),
        vmem((evals, NZ, GROWS, K), F32),
        vmem((reduces, VIEWS, NZ, NY, MAIN, K), BF16),
        vmem((reduces, VIEWS, NZ, MAIN, K), BF16),
        vmem((reduces, VIEWS, NZ, MAIN, K), BF16),
        vmem((reduces, VIEWS, NZ, NY, REST, K), BF16),
        vmem((reduces, VIEWS, NY, REST, K), BF16),
        vmem((reduces, VIEWS, NY, REST, K), BF16),
        *[dma((1,)) for _ in range(11)],
        dma((2, VIEWS, NZ)),
        dma((2, VIEWS)),
        dma((2, VIEWS)),
        dma((2, VIEWS)),
        dma((2, VIEWS)),
        dma((VIEWS, NZ)),
        dma((VIEWS, NZ)),
        dma((VIEWS,)),
        dma((VIEWS, NZ)),
        dma((VIEWS,)),
    ]
    results = pl.pallas_call(
        kernel,
        out_shape=(jax.ShapeDtypeStruct((ROWS, K), F32), jax.ShapeDtypeStruct((VIEWS, OWN, K), F32)),
        in_specs=[pl.BlockSpec(memory_space=pltpu.VMEM)] * 2,
        out_specs=(pl.BlockSpec(memory_space=pltpu.VMEM),) * 2,
        scratch_shapes=scratch,
        compiler_params=pltpu.CompilerParams(collective_id=0, has_side_effects=True, vmem_limit_bytes=56 << 20),
        name="gcca",
    )(view_data, init_coeffs)
    return pl.pallas_call(
        keep,
        out_shape=(jax.ShapeDtypeStruct((ROWS, K), F32), jax.ShapeDtypeStruct((VIEWS, OWN, K), F32)),
        in_specs=[pl.BlockSpec(memory_space=pltpu.VMEM)] * 2,
        out_specs=(pl.BlockSpec(memory_space=pltpu.VMEM),) * 2,
        name="keep",
    )(*results)


def solution(mesh):
    in_specs = (P("view", "samp", None), P("view", None, None))
    out_specs = (P("samp", None), P("view", "samp", None))
    return jax.shard_map(body, mesh=mesh, in_specs=in_specs, out_specs=out_specs, check_vma=False)
```

```python
import functools

import jax
import jax.numpy as jnp
from jax import lax
from jax.experimental import pallas as pl
from jax.experimental.pallas import tpu as pltpu
from jax.sharding import PartitionSpec as P

OUTER = 2
NS_ITERS = 12
RIDGE = 0.1
STEP = 0.5

HIGH = lax.Precision.HIGHEST
MESH = pl.DeviceIdType.MESH
F32 = jnp.float32
BF16 = jnp.bfloat16

NX, NC, NY, NZ = 4, 2, 4, 8
VIEWS, ROWS, FEATS, K = 2, 512, 2048, 128
BLOCK = FEATS // NZ
OWN = BLOCK // NY
MAIN, REST = 48, 16
SAMPLES = ROWS * NY * NZ
PEERS = NX * NC
SENT = (NY * NZ - 1) * OWN * K // ROWS
GROWS = K // (NX * NC)
HALF = ROWS // NC


def dot32(a, b):
    return jnp.dot(a, b, precision=HIGH, preferred_element_type=F32)


def dot16(a, b):
    return jnp.dot(a, b, preferred_element_type=F32)


def halves(a):
    hi = a.astype(BF16)
    return hi, (a - hi.astype(F32)).astype(BF16)


def far_first(i):
    odd = lax.rem(i, 2)
    return lax.rem(4 + odd * ((i + 1) // 2) - (1 - odd) * (i // 2), NZ)


def kernel(
    x_hbm, w_ref, scores_ref, coeffs_ref,
    x_ref, xt, wb, gb, p, pb, sb, wrow, bm, ga, gs,
    cout, cin, xin, summed, gram, gpart, gvin, gyout, gyin, gzout, gzin,
    ryin, szout, rz2in, rz1in, syout, ry2in,
    core_r, core_s, vrs_r, vag_r, gx_r, gy_r, gz_r, gv_r, vrs_s, vag_s, gram_s,
    ry_r, rz2_r, rz1_r, ry2_r, rs_s,
    az_r, ayf_r, ay_r, az2_r, ag_s, load_s,
):
    v = lax.axis_index("view")
    s = lax.axis_index("samp")
    x, core = v // NC, lax.rem(v, NC)
    y, z = lax.rem(s, NY), s // NY
    sibling = {"view": v + 1 - 2 * core, "samp": s}

    def y_peer(m):
        return {"view": v, "samp": z * NY + lax.rem(y + m, NY)}

    def z_peer(j):
        return {"view": v, "samp": lax.rem(z + j, NZ) * NY + y}

    def v_peer(j):
        return {"view": lax.rem(v + j, PEERS), "samp": s}

    def copy(src, dst, send, recv, device):
        return pltpu.make_async_remote_copy(
            src_ref=src, dst_ref=dst, send_sem=send, recv_sem=recv, device_id=device, device_id_type=MESH
        )

    def arrived(ref, recv):
        copy(ref, ref, ag_s.at[0], recv, y_peer(1)).wait_recv()

    def sent(ref, send):
        copy(ref, ref, send, ay_r.at[0], y_peer(1)).wait_send()

    def load(i):
        cols = pl.ds(pl.multiple_of(i * BLOCK, BLOCK), BLOCK)
        return pltpu.make_async_copy(x_hbm.at[:, :, cols], x_ref.at[:, :, cols], load_s.at[i])

    for i in range(NZ):
        load(i).start()

    barrier = pltpu.get_barrier_semaphore()
    for m in range(1, NY):
        pl.semaphore_signal(barrier, inc=1, device_id=y_peer(m), device_id_type=MESH)
    for j in range(1, NZ):
        pl.semaphore_signal(barrier, inc=1, device_id=z_peer(j), device_id_type=MESH)
    for j in range(1, PEERS):
        pl.semaphore_signal(barrier, inc=1, device_id=v_peer(j), device_id_type=MESH)

    def vrs_start(t):
        away = pl.ds(pl.multiple_of((1 - core) * HALF, HALF), HALF)
        cout[t] = p[0, away] + p[1, away]
        copy(cout.at[t], cin.at[t], core_s.at[0], core_r.at[0], sibling).start()

    def vrs_mid(t):
        here = pl.ds(pl.multiple_of(core * HALF, HALF), HALF)
        total = p[0, here] + p[1, here]
        arrived(cin.at[t], core_r.at[0])
        xin[t, x] = (total + cin[t]).astype(BF16)
        for k in (2, 1, 3):
            copy(xin.at[t, x], xin.at[t, x], vrs_s.at[0], vrs_r.at[0], v_peer(2 * k)).start()

    def vrs_end(t):
        here = pl.ds(pl.multiple_of(core * HALF, HALF), HALF)
        arrived(xin.at[t, pl.ds(0, NX - 1)], vrs_r.at[0])
        total = xin[t, 0].astype(F32)
        for k in range(1, NX):
            total = total + xin[t, k].astype(F32)
        summed[t, here] = total
        gpart[t] = dot32(total.T, total).reshape(PEERS, GROWS, K)
        copy(gpart.at[t, v + 1 - 2 * core], gvin.at[t], gram_s.at[0], gx_r.at[0], sibling).start()
        copy(summed.at[t, here], summed.at[t, here], vag_s.at[0], vag_r.at[0], sibling).start()

    def vag_end(t):
        arrived(summed.at[t, pl.ds(0, HALF)], vag_r.at[0])

    def gram_v_end(t):
        arrived(gvin.at[t], gx_r.at[0])
        gyout[t] = gpart[t, v] + gvin[t]
        for m in range(1, NY):
            copy(gyout.at[t], gyin.at[t, m], gram_s.at[0], gy_r.at[0], y_peer(m)).start()

    def gram_y_end(t):
        total = gyout[t]
        arrived(gyin.at[t, pl.ds(1, NY - 1)], gy_r.at[0])
        for m in range(1, NY):
            total = total + gyin[t, m]
        gzout[t] = total
        for j in (4, 5, 3, 6, 2, 7, 1):
            copy(gzout.at[t], gzin.at[t, j], gram_s.at[0], gz_r.at[0], z_peer(j)).start()

    def gram_z_end(t):
        total = gzout[t]
        arrived(gzin.at[t, pl.ds(1, NZ - 1)], gz_r.at[0])
        for j in range(1, NZ):
            total = total + gzin[t, j]
        gram[t, pl.ds(v * GROWS, GROWS)] = total
        block = gram.at[t, pl.ds(v * GROWS, GROWS)]
        for j in range(1, PEERS):
            copy(block, block, gram_s.at[0], gv_r.at[0], v_peer(j)).start()

    def gram_end(t):
        arrived(gram.at[t, pl.ds(0, K - GROWS)], gv_r.at[0])
        sent(cout.at[t], core_s.at[0])
        sent(xin.at[t, pl.ds(0, NX - 1)], vrs_s.at[0])
        sent(summed.at[t, pl.ds(0, HALF)], vag_s.at[0])
        sent(summed.at[t, pl.ds(0, (NY + NZ + PEERS - 2) * GROWS)], gram_s.at[0])

    def eye_mat():
        row = lax.broadcasted_iota(jnp.int32, (K, K), 0)
        col = lax.broadcasted_iota(jnp.int32, (K, K), 1)
        return jnp.where(row == col, 1.0, 0.0).astype(F32)

    def newton_init(t):
        eye = eye_mat()
        full = gram[t]
        trace = jnp.sum(full * eye, keepdims=True)
        shrunk = full + trace / K * eye
        scale = jnp.sqrt(jnp.sum(shrunk * shrunk, keepdims=True))
        return jnp.concatenate([shrunk / scale, eye], axis=1), scale

    def newton_turns(first, last, both, beside=None):
        eye = eye_mat()

        def turn(i, both):
            approx, inverse = both[:, :K], both[:, K:]
            hi, lo = halves(both)
            ah, al, ih, il = hi[:, :K], lo[:, :K], hi[:, K:], lo[:, K:]
            none = jnp.zeros((K, K), BF16)
            left = jnp.concatenate([ih, il], axis=1)
            right = jnp.concatenate([jnp.concatenate([ah, al], axis=1), jnp.concatenate([ah, none], axis=1)], axis=0)
            parts = dot16(left, right)
            factor = 0.5 * (3.0 * eye - (parts[:, :K] + parts[:, K:]))
            fh, fl = halves(factor)
            both = dot16(jnp.concatenate([fh, fl], axis=1), jnp.concatenate([hi, hi], axis=0)) + dot16(fh, lo)
            if beside is not None:
                beside(i)
            return both

        return lax.fori_loop(first, last, turn, both)

    def ry_start(r, q, member, j):
        to_z = lax.rem(z + j, NZ)
        for m in range(1, NY):
            to_y = lax.rem(y + m, NY)
            copy(
                gb.at[r, member, to_z, to_y, pl.ds(0, MAIN)], ryin.at[r, member, j, m],
                rs_s.at[q, member], ry_r.at[q, member, j], y_peer(m),
            ).start()

    def rz1_start(r, q, member, j):
        to_z = lax.rem(z + j, NZ)
        copy(
            gb.at[r, member, to_z, :, pl.ds(MAIN, REST)], rz1in.at[r, member, j],
            rs_s.at[q, member], rz1_r.at[q, member], z_peer(j),
        ).start()

    def rs_start(r, q, member, right, both_orders=True):
        def step(i, _):
            j = far_first(i)
            to_z = lax.rem(z + j, NZ)
            rows = pl.ds(pl.multiple_of(to_z * BLOCK, BLOCK), BLOCK)
            block = dot16(xt[member, rows, :], right())
            gb[r, member, to_z] = block.astype(BF16).reshape(NY, OWN, K)
            ry_start(r, q, member, j)
            if both_orders:

                @pl.when(i < NZ - 1)
                def _():
                    rz1_start(r, q, member, j)

            return 0

        lax.fori_loop(0, NZ, step, 0)

    def rs_other_order(r, q, member):
        for j in (4, 5, 3, 6, 2, 7, 1):
            rz1_start(r, q, member, j)

    def rs_mid_step(r, q, member, i):
        j = far_first(i)
        to_z = lax.rem(z + j, NZ)
        total = gb[r, member, to_z, y, 0:MAIN].astype(F32)
        arrived(ryin.at[r, member, j, pl.ds(1, NY - 1)], ry_r.at[q, member, j])
        for m in range(1, NY):
            total = total + ryin[r, member, j, m].astype(F32)
        szout[r, member, j] = total.astype(BF16)

        @pl.when(i < NZ - 1)
        def _():
            copy(
                szout.at[r, member, j], rz2in.at[r, member, j], rs_s.at[q, member], rz2_r.at[q, member], z_peer(j)
            ).start()

    def rs_mid_rest(r, q, member):
        total = gb[r, member, z, :, MAIN:OWN].astype(F32)
        arrived(rz1in.at[r, member, pl.ds(1, NZ - 1)], rz1_r.at[q, member])
        for j in range(1, NZ):
            total = total + rz1in[r, member, j].astype(F32)
        syout[r, member] = total.astype(BF16)
        for m in range(1, NY):
            to_y = lax.rem(y + m, NY)
            copy(
                syout.at[r, member, to_y], ry2in.at[r, member, m], rs_s.at[q, member], ry2_r.at[q, member], y_peer(m)
            ).start()

    def rs_mid(r, q, member):
        def step(i, _):
            rs_mid_step(r, q, member, i)
            return 0

        lax.fori_loop(0, NZ, step, 0)
        rs_mid_rest(r, q, member)

    def rs_end(r, q, member, out):
        total = syout[r, member, y].astype(F32)
        arrived(ry2in.at[r, member, pl.ds(1, NY - 1)], ry2_r.at[q, member])
        for m in range(1, NY):
            total = total + ry2in[r, member, m].astype(F32)
        out[member, MAIN:OWN] = total
        total = szout[r, member, 0].astype(F32)
        arrived(rz2in.at[r, member, pl.ds(1, NZ - 1)], rz2_r.at[q, member])
        for j in range(1, NZ):
            total = total + rz2in[r, member, j].astype(F32)
        out[member, 0:MAIN] = total
        sent(xt.at[0, pl.ds(0, SENT)], rs_s.at[q, member])

    def ayf_start(a, member, j):
        from_z = lax.rem(z - j + NZ, NZ)
        block = wb.at[a, member, from_z, y, pl.ds(0, MAIN)]
        for m in range(1, NY):
            copy(block, block, ag_s.at[member], ayf_r.at[member, j], y_peer(m)).start()

    def gather_start(a, member):
        wb[a, member, z, y] = wrow[member].astype(BF16)
        block = wb.at[a, member, z, y, pl.ds(MAIN, REST)]
        for m in range(1, NY):
            copy(block, block, ag_s.at[member], ay_r.at[member], y_peer(m)).start()
        ayf_start(a, member, 0)
        block = wb.at[a, member, z, y, pl.ds(0, MAIN)]
        for j in (1, 7, 2, 6, 3, 5, 4):
            copy(block, block, ag_s.at[member], az_r.at[member, j], z_peer(j)).start()

    def gather_forward(a, member):
        arrived(wb.at[a, member, z, pl.ds(0, NY - 1), pl.ds(0, REST)], ay_r.at[member])
        block = wb.at[a, member, z, :, pl.ds(MAIN, REST)]
        for j in (1, 7, 2, 6, 3, 5, 4):
            copy(block, block, ag_s.at[member], az2_r.at[member, j], z_peer(j)).start()

        def forward(i, _):
            j = far_first(NZ - 1 - i)
            arrived(wb.at[a, member, z, y, pl.ds(0, MAIN)], az_r.at[member, j])
            ayf_start(a, member, j)
            return 0

        lax.fori_loop(1, NZ, forward, 0)

    def gather_products(a, member):
        p[member] = jnp.zeros((ROWS, K), F32)

        def product(i, _):
            j = far_first(NZ - 1 - i)
            from_z = lax.rem(z - j + NZ, NZ)
            arrived(wb.at[a, member, z, pl.ds(0, NY - 1), pl.ds(0, MAIN)], ayf_r.at[member, j])

            @pl.when(i > 0)
            def _():
                arrived(wb.at[a, member, z, :, pl.ds(0, REST)], az2_r.at[member, j])

            product_of(a, member, from_z)
            return 0

        lax.fori_loop(0, NZ, product, 0)
        sent(xt.at[0, pl.ds(0, SENT)], ag_s.at[member])

    def product_of(a, member, from_z):
        cols = pl.ds(pl.multiple_of(from_z * BLOCK, BLOCK), BLOCK)
        p[member] += dot16(x_ref[member, :, cols], wb[a, member, from_z].reshape(BLOCK, K))

    def update(member):
        grad = (ga[member] - bm[member]) / SAMPLES
        wrow[member] = wrow[member] - STEP * (grad + RIDGE * wrow[member])

    wb[0] = w_ref[...].reshape(VIEWS, NZ, NY, OWN, K).astype(BF16)
    wrow[...] = w_ref[:, pl.ds(pl.multiple_of(s * OWN, OWN), OWN), :]
    p[...] = jnp.zeros_like(p)

    def first(i, _):
        load(i).wait()
        cols = pl.ds(pl.multiple_of(i * BLOCK, BLOCK), BLOCK)
        for member in range(VIEWS):
            product_of(0, member, i)
            xt[member, cols, :] = x_ref[member, :, cols].T
        return 0

    lax.fori_loop(0, NZ, first, 0, unroll=2)
    pl.semaphore_wait(barrier, (NY - 1) + (NZ - 1) + (PEERS - 1))

    def outer(o, _):
        own_r, sum_r, next_r = 3 * o, 3 * o + 1, 3 * o + 2
        one, two = 2 * o + 1, 2 * o + 2
        vrs_start(o)
        pb[0] = p[0].astype(BF16)
        rs_start(own_r, 0, 0, lambda: pb[0])
        vrs_mid(o)
        pb[1] = p[1].astype(BF16)
        rs_start(own_r, 0, 1, lambda: pb[1])
        vrs_end(o)
        gram_v_end(o)
        rs_mid(own_r, 0, 0)
        rs_mid(own_r, 0, 1)
        vag_end(o)
        sb[...] = summed[o].astype(BF16)
        rs_start(sum_r, 1, 0, lambda: sb[...], both_orders=False)
        gram_y_end(o)
        rs_other_order(sum_r, 1, 0)
        rs_start(sum_r, 1, 1, lambda: sb[...], both_orders=False)
        rs_other_order(sum_r, 1, 1)
        gram_z_end(o)
        rs_end(own_r, 0, 0, ga)
        rs_end(own_r, 0, 1, ga)
        rs_mid(sum_r, 1, 0)
        gram_end(o)
        both, scale = newton_init(o)
        both = newton_turns(0, NZ, both, lambda i: rs_mid_step(sum_r, 1, 1, i))
        rs_mid_rest(sum_r, 1, 1)
        both = newton_turns(NZ, NS_ITERS, both)
        white = both[:, K:] * jnp.sqrt(SAMPLES / scale)
        for member in range(VIEWS):
            rs_end(sum_r, 1, member, gs)
            bm[member] = dot32(gs[member], white)
            update(member)
            gather_start(one, member)
        for member in range(VIEWS):
            gather_forward(one, member)
        for member in range(VIEWS):
            gather_products(one, member)
            pb[member] = p[member].astype(BF16)
            rs_start(next_r, 0, member, lambda: pb[member])
        for member in range(VIEWS):
            rs_mid(next_r, 0, member)
        for member in range(VIEWS):
            rs_end(next_r, 0, member, ga)
            update(member)
            gather_start(two, member)
        for member in range(VIEWS):
            gather_forward(two, member)
        for member in range(VIEWS):
            gather_products(two, member)
        return 0

    lax.fori_loop(0, OUTER, outer, 0)
    vrs_start(OUTER)
    coeffs_ref[...] = wrow[...]
    vrs_mid(OUTER)
    vrs_end(OUTER)
    gram_v_end(OUTER)
    gram_y_end(OUTER)
    gram_z_end(OUTER)
    vag_end(OUTER)
    gram_end(OUTER)
    both, scale = newton_init(OUTER)
    both = newton_turns(0, NS_ITERS, both)
    scores_ref[...] = dot32(summed[OUTER], both[:, K:] * jnp.sqrt(SAMPLES / scale))


def keep(scores_ref, coeffs_ref, scores_out, coeffs_out):
    scores_out[...] = scores_ref[...]
    coeffs_out[...] = coeffs_ref[...]


def body(view_data, init_coeffs):
    evals, reduces, gathers = OUTER + 1, 3 * OUTER, 2 * OUTER
    vmem, dma = pltpu.VMEM, pltpu.SemaphoreType.DMA
    scratch = [
        vmem((VIEWS, ROWS, FEATS), BF16),
        vmem((VIEWS, FEATS, ROWS), BF16),
        vmem((gathers + 1, VIEWS, NZ, NY, OWN, K), BF16),
        vmem((reduces, VIEWS, NZ, NY, OWN, K), BF16),
        vmem((VIEWS, ROWS, K), F32),
        vmem((VIEWS, ROWS, K), BF16),
        vmem((ROWS, K), BF16),
        vmem((VIEWS, OWN, K), F32),
        vmem((VIEWS, OWN, K), F32),
        vmem((VIEWS, OWN, K), F32),
        vmem((VIEWS, OWN, K), F32),
        vmem((evals, HALF, K), F32),
        vmem((evals, HALF, K), F32),
        vmem((evals, NX, HALF, K), BF16),
        vmem((evals, ROWS, K), F32),
        vmem((evals, K, K), F32),
        vmem((evals, PEERS, GROWS, K), F32),
        vmem((evals, GROWS, K), F32),
        vmem((evals, GROWS, K), F32),
        vmem((evals, NY, GROWS, K), F32),
        vmem((evals, GROWS, K), F32),
        vmem((evals, NZ, GROWS, K), F32),
        vmem((reduces, VIEWS, NZ, NY, MAIN, K), BF16),
        vmem((reduces, VIEWS, NZ, MAIN, K), BF16),
        vmem((reduces, VIEWS, NZ, MAIN, K), BF16),
        vmem((reduces, VIEWS, NZ, NY, REST, K), BF16),
        vmem((reduces, VIEWS, NY, REST, K), BF16),
        vmem((reduces, VIEWS, NY, REST, K), BF16),
        *[dma((1,)) for _ in range(11)],
        dma((2, VIEWS, NZ)),
        dma((2, VIEWS)),
        dma((2, VIEWS)),
        dma((2, VIEWS)),
        dma((2, VIEWS)),
        dma((VIEWS, NZ)),
        dma((VIEWS, NZ)),
        dma((VIEWS,)),
        dma((VIEWS, NZ)),
        dma((VIEWS,)),
        dma((NZ,)),
    ]
    results = pl.pallas_call(
        kernel,
        out_shape=(jax.ShapeDtypeStruct((ROWS, K), F32), jax.ShapeDtypeStruct((VIEWS, OWN, K), F32)),
        in_specs=[pl.BlockSpec(memory_space=pl.ANY), pl.BlockSpec(memory_space=pltpu.VMEM)],
        out_specs=(pl.BlockSpec(memory_space=pltpu.VMEM),) * 2,
        scratch_shapes=scratch,
        compiler_params=pltpu.CompilerParams(collective_id=0, has_side_effects=True, vmem_limit_bytes=56 << 20),
        name="gcca",
    )(view_data, init_coeffs)
    return pl.pallas_call(
        keep,
        out_shape=(jax.ShapeDtypeStruct((ROWS, K), F32), jax.ShapeDtypeStruct((VIEWS, OWN, K), F32)),
        in_specs=[pl.BlockSpec(memory_space=pltpu.VMEM)] * 2,
        out_specs=(pl.BlockSpec(memory_space=pltpu.VMEM),) * 2,
        name="keep",
    )(*results)


def solution(mesh):
    in_specs = (P("view", "samp", None), P("view", None, None))
    out_specs = (P("samp", None), P("view", "samp", None))
    return jax.shard_map(body, mesh=mesh, in_specs=in_specs, out_specs=out_specs, check_vma=False)
```

```python
import functools

import jax
import jax.numpy as jnp
from jax import lax
from jax.experimental import pallas as pl
from jax.experimental.pallas import tpu as pltpu
from jax.sharding import PartitionSpec as P

OUTER = 2
NS_ITERS = 12
RIDGE = 0.1
STEP = 0.5

HIGH = lax.Precision.HIGHEST
MESH = pl.DeviceIdType.MESH
F32 = jnp.float32
BF16 = jnp.bfloat16

NX, NC, NY, NZ = 4, 2, 4, 8
VIEWS, ROWS, FEATS, K = 2, 512, 2048, 128
BLOCK = FEATS // NZ
OWN = BLOCK // NY
MAIN, REST = 48, 16
SAMPLES = ROWS * NY * NZ
PEERS = NX * NC
SENT = (NY * NZ - 1) * OWN * K // ROWS
GROWS = K // (NX * NC)
HALF = ROWS // NC


def dot32(a, b):
    return jnp.dot(a, b, precision=HIGH, preferred_element_type=F32)


def dot16(a, b):
    return jnp.dot(a, b, preferred_element_type=F32)


def halves(a):
    hi = a.astype(BF16)
    return hi, (a - hi.astype(F32)).astype(BF16)


def far_first(i):
    odd = lax.rem(i, 2)
    return lax.rem(4 + odd * ((i + 1) // 2) - (1 - odd) * (i // 2), NZ)


def kernel(
    x_hbm, w_ref, scores_ref, coeffs_ref,
    x_ref, xt, wb, gb, p, pb, sb, wrow, bm, ga, gs,
    cout, cin, xin, summed, gram, gpart, gvin, gyout, gyin, gzout, gzin,
    ryin, szout, rz2in, rz1in, syout, ry2in,
    core_r, core_s, vrs_r, vag_r, gx_r, gy_r, gz_r, gv_r, vrs_s, vag_s, gram_s,
    ry_r, rz2_r, rz1_r, ry2_r, rs_s,
    az_r, ayf_r, ay_r, az2_r, ag_s, load_s,
):
    v = lax.axis_index("view")
    s = lax.axis_index("samp")
    x, core = v // NC, lax.rem(v, NC)
    y, z = lax.rem(s, NY), s // NY
    sibling = {"view": v + 1 - 2 * core, "samp": s}

    def y_peer(m):
        return {"view": v, "samp": z * NY + lax.rem(y + m, NY)}

    def z_peer(j):
        return {"view": v, "samp": lax.rem(z + j, NZ) * NY + y}

    def v_peer(j):
        return {"view": lax.rem(v + j, PEERS), "samp": s}

    def copy(src, dst, send, recv, device):
        return pltpu.make_async_remote_copy(
            src_ref=src, dst_ref=dst, send_sem=send, recv_sem=recv, device_id=device, device_id_type=MESH
        )

    def arrived(ref, recv):
        copy(ref, ref, ag_s.at[0], recv, y_peer(1)).wait_recv()

    def sent(ref, send):
        copy(ref, ref, send, ay_r.at[0], y_peer(1)).wait_send()

    def load(i):
        cols = pl.ds(pl.multiple_of(i * BLOCK, BLOCK), BLOCK)
        return pltpu.make_async_copy(x_hbm.at[:, :, cols], x_ref.at[:, :, cols], load_s.at[i])

    for i in range(NZ):
        load(i).start()

    barrier = pltpu.get_barrier_semaphore()
    for m in range(1, NY):
        pl.semaphore_signal(barrier, inc=1, device_id=y_peer(m), device_id_type=MESH)
    for j in range(1, NZ):
        pl.semaphore_signal(barrier, inc=1, device_id=z_peer(j), device_id_type=MESH)
    for j in range(1, PEERS):
        pl.semaphore_signal(barrier, inc=1, device_id=v_peer(j), device_id_type=MESH)

    def vrs_start(t):
        away = pl.ds(pl.multiple_of((1 - core) * HALF, HALF), HALF)
        cout[t] = p[0, away] + p[1, away]
        copy(cout.at[t], cin.at[t], core_s.at[0], core_r.at[0], sibling).start()

    def vrs_mid(t):
        here = pl.ds(pl.multiple_of(core * HALF, HALF), HALF)
        total = p[0, here] + p[1, here]
        arrived(cin.at[t], core_r.at[0])
        xin[t, x] = (total + cin[t]).astype(BF16)
        for k in (2, 1, 3):
            copy(xin.at[t, x], xin.at[t, x], vrs_s.at[0], vrs_r.at[0], v_peer(2 * k)).start()

    def vrs_end(t):
        here = pl.ds(pl.multiple_of(core * HALF, HALF), HALF)
        arrived(xin.at[t, pl.ds(0, NX - 1)], vrs_r.at[0])
        total = xin[t, 0].astype(F32)
        for k in range(1, NX):
            total = total + xin[t, k].astype(F32)
        summed[t, here] = total
        gpart[t] = dot32(total.T, total).reshape(PEERS, GROWS, K)
        copy(gpart.at[t, v + 1 - 2 * core], gvin.at[t], gram_s.at[0], gx_r.at[0], sibling).start()
        copy(summed.at[t, here], summed.at[t, here], vag_s.at[0], vag_r.at[0], sibling).start()

    def vag_end(t):
        arrived(summed.at[t, pl.ds(0, HALF)], vag_r.at[0])

    def gram_v_end(t):
        arrived(gvin.at[t], gx_r.at[0])
        gyout[t] = gpart[t, v] + gvin[t]
        for m in range(1, NY):
            copy(gyout.at[t], gyin.at[t, m], gram_s.at[0], gy_r.at[0], y_peer(m)).start()

    def gram_y_end(t):
        total = gyout[t]
        arrived(gyin.at[t, pl.ds(1, NY - 1)], gy_r.at[0])
        for m in range(1, NY):
            total = total + gyin[t, m]
        gzout[t] = total
        for j in (4, 5, 3, 6, 2, 7, 1):
            copy(gzout.at[t], gzin.at[t, j], gram_s.at[0], gz_r.at[0], z_peer(j)).start()

    def gram_z_end(t):
        total = gzout[t]
        arrived(gzin.at[t, pl.ds(1, NZ - 1)], gz_r.at[0])
        for j in range(1, NZ):
            total = total + gzin[t, j]
        gram[t, pl.ds(v * GROWS, GROWS)] = total
        block = gram.at[t, pl.ds(v * GROWS, GROWS)]
        for j in range(1, PEERS):
            copy(block, block, gram_s.at[0], gv_r.at[0], v_peer(j)).start()

    def gram_end(t):
        arrived(gram.at[t, pl.ds(0, K - GROWS)], gv_r.at[0])
        sent(cout.at[t], core_s.at[0])
        sent(xin.at[t, pl.ds(0, NX - 1)], vrs_s.at[0])
        sent(summed.at[t, pl.ds(0, HALF)], vag_s.at[0])
        sent(summed.at[t, pl.ds(0, (NY + NZ + PEERS - 2) * GROWS)], gram_s.at[0])

    def eye_mat():
        row = lax.broadcasted_iota(jnp.int32, (K, K), 0)
        col = lax.broadcasted_iota(jnp.int32, (K, K), 1)
        return jnp.where(row == col, 1.0, 0.0).astype(F32)

    def newton_init(t):
        eye = eye_mat()
        full = gram[t]
        trace = jnp.sum(full * eye, keepdims=True)
        shrunk = full + trace / K * eye
        scale = jnp.sqrt(jnp.sum(shrunk * shrunk, keepdims=True))
        return jnp.concatenate([shrunk / scale, eye], axis=1), scale

    def newton_turns(first, last, both, beside=None):
        eye = eye_mat()

        def turn(i, both):
            approx, inverse = both[:, :K], both[:, K:]
            hi, lo = halves(both)
            ah, al, ih, il = hi[:, :K], lo[:, :K], hi[:, K:], lo[:, K:]
            none = jnp.zeros((K, K), BF16)
            left = jnp.concatenate([ih, il], axis=1)
            right = jnp.concatenate([jnp.concatenate([ah, al], axis=1), jnp.concatenate([ah, none], axis=1)], axis=0)
            parts = dot16(left, right)
            factor = 0.5 * (3.0 * eye - (parts[:, :K] + parts[:, K:]))
            fh, fl = halves(factor)
            both = dot16(jnp.concatenate([fh, fl], axis=1), jnp.concatenate([hi, hi], axis=0)) + dot16(fh, lo)
            if beside is not None:
                beside(i)
            return both

        return lax.fori_loop(first, last, turn, both)

    def ry_start(r, q, member, j):
        to_z = lax.rem(z + j, NZ)
        for m in (2, 1, 3):
            to_y = lax.rem(y + m, NY)
            copy(
                gb.at[r, member, to_z, to_y, pl.ds(0, MAIN)], ryin.at[r, member, j, m],
                rs_s.at[q, member], ry_r.at[q, member, j], y_peer(m),
            ).start()

    def rz1_start(r, q, member, j):
        to_z = lax.rem(z + j, NZ)
        copy(
            gb.at[r, member, to_z, :, pl.ds(MAIN, REST)], rz1in.at[r, member, j],
            rs_s.at[q, member], rz1_r.at[q, member], z_peer(j),
        ).start()

    def rs_start(r, q, member, right, both_orders=True):
        def step(i, _):
            j = far_first(i)
            to_z = lax.rem(z + j, NZ)
            rows = pl.ds(pl.multiple_of(to_z * BLOCK, BLOCK), BLOCK)
            block = dot16(xt[member, rows, :], right())
            gb[r, member, to_z] = block.astype(BF16).reshape(NY, OWN, K)
            ry_start(r, q, member, j)
            if both_orders:

                @pl.when(i < NZ - 1)
                def _():
                    rz1_start(r, q, member, j)

            return 0

        lax.fori_loop(0, NZ, step, 0)

    def rs_other_order(r, q, member):
        for j in (4, 5, 3, 6, 2, 7, 1):
            rz1_start(r, q, member, j)

    def rs_mid_step(r, q, member, i):
        j = far_first(i)
        to_z = lax.rem(z + j, NZ)
        total = gb[r, member, to_z, y, 0:MAIN].astype(F32)
        arrived(ryin.at[r, member, j, pl.ds(1, NY - 1)], ry_r.at[q, member, j])
        for m in range(1, NY):
            total = total + ryin[r, member, j, m].astype(F32)
        szout[r, member, j] = total.astype(BF16)

        @pl.when(i < NZ - 1)
        def _():
            copy(
                szout.at[r, member, j], rz2in.at[r, member, j], rs_s.at[q, member], rz2_r.at[q, member], z_peer(j)
            ).start()

    def rs_mid_rest(r, q, member):
        total = gb[r, member, z, :, MAIN:OWN].astype(F32)
        arrived(rz1in.at[r, member, pl.ds(1, NZ - 1)], rz1_r.at[q, member])
        for j in range(1, NZ):
            total = total + rz1in[r, member, j].astype(F32)
        syout[r, member] = total.astype(BF16)
        for m in range(1, NY):
            to_y = lax.rem(y + m, NY)
            copy(
                syout.at[r, member, to_y], ry2in.at[r, member, m], rs_s.at[q, member], ry2_r.at[q, member], y_peer(m)
            ).start()

    def rs_mid(r, q, member):
        def step(i, _):
            rs_mid_step(r, q, member, i)
            return 0

        lax.fori_loop(0, NZ, step, 0)
        rs_mid_rest(r, q, member)

    def rs_end(r, q, member, out):
        total = syout[r, member, y].astype(F32)
        arrived(ry2in.at[r, member, pl.ds(1, NY - 1)], ry2_r.at[q, member])
        for m in range(1, NY):
            total = total + ry2in[r, member, m].astype(F32)
        out[member, MAIN:OWN] = total
        total = szout[r, member, 0].astype(F32)
        arrived(rz2in.at[r, member, pl.ds(1, NZ - 1)], rz2_r.at[q, member])
        for j in range(1, NZ):
            total = total + rz2in[r, member, j].astype(F32)
        out[member, 0:MAIN] = total
        sent(xt.at[0, pl.ds(0, SENT)], rs_s.at[q, member])

    def ayf_start(a, member, j):
        from_z = lax.rem(z - j + NZ, NZ)
        block = wb.at[a, member, from_z, y, pl.ds(0, MAIN)]
        for m in (2, 1, 3):
            copy(block, block, ag_s.at[member], ayf_r.at[member, j], y_peer(m)).start()

    def gather_start(a, member):
        wb[a, member, z, y] = wrow[member].astype(BF16)
        block = wb.at[a, member, z, y, pl.ds(MAIN, REST)]
        for m in range(1, NY):
            copy(block, block, ag_s.at[member], ay_r.at[member], y_peer(m)).start()
        ayf_start(a, member, 0)
        block = wb.at[a, member, z, y, pl.ds(0, MAIN)]
        for j in (1, 7, 2, 6, 3, 5, 4):
            copy(block, block, ag_s.at[member], az_r.at[member, j], z_peer(j)).start()

    def gather_forward(a, member):
        arrived(wb.at[a, member, z, pl.ds(0, NY - 1), pl.ds(0, REST)], ay_r.at[member])
        block = wb.at[a, member, z, :, pl.ds(MAIN, REST)]
        for j in (1, 7, 2, 6, 3, 5, 4):
            copy(block, block, ag_s.at[member], az2_r.at[member, j], z_peer(j)).start()

        def forward(i, _):
            j = far_first(NZ - 1 - i)
            arrived(wb.at[a, member, z, y, pl.ds(0, MAIN)], az_r.at[member, j])
            ayf_start(a, member, j)
            return 0

        lax.fori_loop(1, NZ, forward, 0)

    def gather_products(a, member):
        p[member] = jnp.zeros((ROWS, K), F32)

        def product(i, _):
            j = far_first(NZ - 1 - i)
            from_z = lax.rem(z - j + NZ, NZ)
            arrived(wb.at[a, member, z, pl.ds(0, NY - 1), pl.ds(0, MAIN)], ayf_r.at[member, j])

            @pl.when(i > 0)
            def _():
                arrived(wb.at[a, member, z, :, pl.ds(0, REST)], az2_r.at[member, j])

            product_of(a, member, from_z)
            return 0

        lax.fori_loop(0, NZ, product, 0)
        sent(xt.at[0, pl.ds(0, SENT)], ag_s.at[member])

    def product_of(a, member, from_z):
        cols = pl.ds(pl.multiple_of(from_z * BLOCK, BLOCK), BLOCK)
        p[member] += dot16(x_ref[member, :, cols], wb[a, member, from_z].reshape(BLOCK, K))

    def update(member):
        grad = (ga[member] - bm[member]) / SAMPLES
        wrow[member] = wrow[member] - STEP * (grad + RIDGE * wrow[member])

    wb[0] = w_ref[...].reshape(VIEWS, NZ, NY, OWN, K).astype(BF16)
    wrow[...] = w_ref[:, pl.ds(pl.multiple_of(s * OWN, OWN), OWN), :]
    p[...] = jnp.zeros_like(p)

    def first(i, _):
        load(i).wait()
        cols = pl.ds(pl.multiple_of(i * BLOCK, BLOCK), BLOCK)
        for member in range(VIEWS):
            product_of(0, member, i)
            xt[member, cols, :] = x_ref[member, :, cols].T
        return 0

    lax.fori_loop(0, NZ, first, 0, unroll=2)
    pl.semaphore_wait(barrier, (NY - 1) + (NZ - 1) + (PEERS - 1))

    def outer(o, _):
        own_r, sum_r, next_r = 3 * o, 3 * o + 1, 3 * o + 2
        one, two = 2 * o + 1, 2 * o + 2
        vrs_start(o)
        pb[0] = p[0].astype(BF16)
        rs_start(own_r, 0, 0, lambda: pb[0])
        vrs_mid(o)
        pb[1] = p[1].astype(BF16)
        rs_start(own_r, 0, 1, lambda: pb[1])
        vrs_end(o)
        gram_v_end(o)
        rs_mid(own_r, 0, 0)
        rs_mid(own_r, 0, 1)
        vag_end(o)
        sb[...] = summed[o].astype(BF16)
        rs_start(sum_r, 1, 0, lambda: sb[...], both_orders=False)
        gram_y_end(o)
        rs_other_order(sum_r, 1, 0)
        rs_start(sum_r, 1, 1, lambda: sb[...], both_orders=False)
        rs_other_order(sum_r, 1, 1)
        gram_z_end(o)
        rs_end(own_r, 0, 0, ga)
        rs_end(own_r, 0, 1, ga)
        rs_mid(sum_r, 1, 0)
        gram_end(o)
        both, scale = newton_init(o)
        both = newton_turns(0, NZ, both, lambda i: rs_mid_step(sum_r, 1, 1, i))
        rs_mid_rest(sum_r, 1, 1)
        both = newton_turns(NZ, NS_ITERS, both)
        white = both[:, K:] * jnp.sqrt(SAMPLES / scale)
        for member in range(VIEWS):
            rs_end(sum_r, 1, member, gs)
            bm[member] = dot32(gs[member], white)
            update(member)
            gather_start(one, member)
        for member in range(VIEWS):
            gather_forward(one, member)
        for member in range(VIEWS):
            gather_products(one, member)
            pb[member] = p[member].astype(BF16)
            rs_start(next_r, 0, member, lambda: pb[member])
        for member in range(VIEWS):
            rs_mid(next_r, 0, member)
        for member in range(VIEWS):
            rs_end(next_r, 0, member, ga)
            update(member)
            gather_start(two, member)
        for member in range(VIEWS):
            gather_forward(two, member)
        for member in range(VIEWS):
            gather_products(two, member)
        return 0

    lax.fori_loop(0, OUTER, outer, 0)
    vrs_start(OUTER)
    coeffs_ref[...] = wrow[...]
    vrs_mid(OUTER)
    vrs_end(OUTER)
    gram_v_end(OUTER)
    gram_y_end(OUTER)
    gram_z_end(OUTER)
    vag_end(OUTER)
    gram_end(OUTER)
    both, scale = newton_init(OUTER)
    both = newton_turns(0, NS_ITERS, both)
    scores_ref[...] = dot32(summed[OUTER], both[:, K:] * jnp.sqrt(SAMPLES / scale))


def keep(scores_ref, coeffs_ref, scores_out, coeffs_out):
    scores_out[...] = scores_ref[...]
    coeffs_out[...] = coeffs_ref[...]


def body(view_data, init_coeffs):
    evals, reduces, gathers = OUTER + 1, 3 * OUTER, 2 * OUTER
    vmem, dma = pltpu.VMEM, pltpu.SemaphoreType.DMA
    scratch = [
        vmem((VIEWS, ROWS, FEATS), BF16),
        vmem((VIEWS, FEATS, ROWS), BF16),
        vmem((gathers + 1, VIEWS, NZ, NY, OWN, K), BF16),
        vmem((reduces, VIEWS, NZ, NY, OWN, K), BF16),
        vmem((VIEWS, ROWS, K), F32),
        vmem((VIEWS, ROWS, K), BF16),
        vmem((ROWS, K), BF16),
        vmem((VIEWS, OWN, K), F32),
        vmem((VIEWS, OWN, K), F32),
        vmem((VIEWS, OWN, K), F32),
        vmem((VIEWS, OWN, K), F32),
        vmem((evals, HALF, K), F32),
        vmem((evals, HALF, K), F32),
        vmem((evals, NX, HALF, K), BF16),
        vmem((evals, ROWS, K), F32),
        vmem((evals, K, K), F32),
        vmem((evals, PEERS, GROWS, K), F32),
        vmem((evals, GROWS, K), F32),
        vmem((evals, GROWS, K), F32),
        vmem((evals, NY, GROWS, K), F32),
        vmem((evals, GROWS, K), F32),
        vmem((evals, NZ, GROWS, K), F32),
        vmem((reduces, VIEWS, NZ, NY, MAIN, K), BF16),
        vmem((reduces, VIEWS, NZ, MAIN, K), BF16),
        vmem((reduces, VIEWS, NZ, MAIN, K), BF16),
        vmem((reduces, VIEWS, NZ, NY, REST, K), BF16),
        vmem((reduces, VIEWS, NY, REST, K), BF16),
        vmem((reduces, VIEWS, NY, REST, K), BF16),
        *[dma((1,)) for _ in range(11)],
        dma((2, VIEWS, NZ)),
        dma((2, VIEWS)),
        dma((2, VIEWS)),
        dma((2, VIEWS)),
        dma((2, VIEWS)),
        dma((VIEWS, NZ)),
        dma((VIEWS, NZ)),
        dma((VIEWS,)),
        dma((VIEWS, NZ)),
        dma((VIEWS,)),
        dma((NZ,)),
    ]
    results = pl.pallas_call(
        kernel,
        out_shape=(jax.ShapeDtypeStruct((ROWS, K), F32), jax.ShapeDtypeStruct((VIEWS, OWN, K), F32)),
        in_specs=[pl.BlockSpec(memory_space=pl.ANY), pl.BlockSpec(memory_space=pltpu.VMEM)],
        out_specs=(pl.BlockSpec(memory_space=pltpu.VMEM),) * 2,
        scratch_shapes=scratch,
        compiler_params=pltpu.CompilerParams(collective_id=0, has_side_effects=True, vmem_limit_bytes=56 << 20),
        name="gcca",
    )(view_data, init_coeffs)
    return pl.pallas_call(
        keep,
        out_shape=(jax.ShapeDtypeStruct((ROWS, K), F32), jax.ShapeDtypeStruct((VIEWS, OWN, K), F32)),
        in_specs=[pl.BlockSpec(memory_space=pltpu.VMEM)] * 2,
        out_specs=(pl.BlockSpec(memory_space=pltpu.VMEM),) * 2,
        name="keep",
    )(*results)


def solution(mesh):
    in_specs = (P("view", "samp", None), P("view", None, None))
    out_specs = (P("samp", None), P("view", "samp", None))
    return jax.shard_map(body, mesh=mesh, in_specs=in_specs, out_specs=out_specs, check_vma=False)
```
